32 devices in a mesh: seq: 8 (over z, y), ch: 4 (over x, core).
Axes of the slice: x: 2, y: 2, z: 4, core: 2. Of those that a mesh axis runs over, the one named last changes fastest.
Arguments:
- query_proj: bfloat16 [2048, 8192], P('seq', 'ch'), may hold values from -6 to 6
- key_proj: bfloat16 [2048, 8192], P('seq', 'ch'), may hold values from -6 to 6
- value_proj: bfloat16 [2048, 8192], P('seq', 'ch'), may hold values from -6 to 6
- decay_rate: float32 [16, 8192], P(None, 'ch'), may hold values from 9.765625e-06 to 0.033
- pole_angle: float32 [16, 8192], P(None, 'ch'), may hold values from -3.140625 to 3.140625
- residue_real: float32 [16, 8192], P(None, 'ch'), may hold values from -6 to 6
- residue_imag: float32 [16, 8192], P(None, 'ch'), may hold values from -6 to 6
- skip_gain: float32 [8192], P('ch'), may hold values from -6 to 6
- norm_gain: float32 [8192], P('ch'), may hold values from 0.5 to 1.5
Outputs:
- layer_out: bfloat16 [2048, 8192], P('seq', 'ch')
The draws below stay inside these ranges and needn't reach their ends.
All inputs are finite; a program needn't handle non-finite values.
Results may differ from the reference program's by a relative error of at most 0.0017.
Values sent between devices are 32-bit elements; how exact they have to be, the bound alone decides.
No kernel may reach another device: no remote copies, remote signals or barrier semaphores. Data moves between devices by JAX's collectives and lax.ppermute only.
A program may use at most 64 MiB of HBM per device.

```python
import math
import jax
import jax.numpy as jnp
from jax import lax

D = 8192
MODES = 16
TOKENS = 2048


def shard_levels(own_key, dims, pieces, low, high):
    def one(position, parts):
        steps = jax.random.uniform(jax.random.fold_in(jax.random.fold_in(own_key, 6), position), (parts,), jnp.float32, low / len(pieces), high / len(pieces))
        return jnp.repeat(jnp.exp(steps), dims[position] // parts).reshape((-1,) + (1,) * (len(dims) - position - 1))

    gain = one(*pieces[0])
    for cut in pieces[1:]:
        gain = gain * one(*cut)
    return gain


def normal_values(stream_key, shape, width, reach, split=(), held_as=jnp.bfloat16):
    array = jax.random.normal(stream_key, shape, jnp.float32) * width
    if len(split) > 0:
        array = shard_levels(stream_key, shape, split, -0.22, 0.18) * array
    return jnp.clip(array, min=-reach, max=reach).astype(held_as)


def setup_inputs(seed: int = 0) -> dict:
    key_list = jax.random.split(jax.random.key(seed), 10)
    return {
        "query_proj": normal_values(key_list[0], (TOKENS, D), 1.0, 6.0, ((0, 8), (1, 4))),
        "key_proj": normal_values(key_list[1], (TOKENS, D), 1.0, 6.0, ((0, 8), (1, 4))),
        "value_proj": normal_values(key_list[2], (TOKENS, D), 1.0, 6.0, ((0, 8), (1, 4))),
        "decay_rate": jnp.clip(jnp.exp(math.log(0.033) - 8.125394 * jax.random.uniform(key_list[3], (MODES, D), jnp.float32) ** shard_levels(key_list[3], (MODES, D), ((1, 4),), -0.2, 0.2)), 9.765624781721272e-06, 0.033),
        "pole_angle": jnp.clip(jax.random.uniform(key_list[4], (MODES, D), jnp.float32, -3.140625, 3.140625), -3.140625, 3.140625),
        "residue_real": normal_values(key_list[5], (MODES, D), 1.0, 6.0, ((1, 4),), jnp.float32),
        "residue_imag": normal_values(key_list[6], (MODES, D), 1.0, 6.0, ((1, 4),), jnp.float32),
        "skip_gain": normal_values(key_list[7], (D,), 1.0, 6.0, ((0, 4),), jnp.float32),
        "norm_gain": jnp.clip(1.0 + 0.1 * jax.random.normal(key_list[8], (D,), jnp.float32), 0.5, 1.5),
    }


def powers(decay_rate, pole_angle, count):
    magnitude = jnp.exp(-count * decay_rate)
    return (magnitude * jnp.cos(count * pole_angle), magnitude * jnp.sin(count * pole_angle))

def reference(query_proj, key_proj, value_proj, decay_rate, pole_angle, residue_real, residue_imag, skip_gain, norm_gain):
    highest = lax.Precision.HIGHEST
    mixed = key_proj.astype(jnp.float32) * value_proj.astype(jnp.float32)
    block_len = 64
    offsets = jnp.arange(block_len).astype(jnp.float32)[:, None, None]
    weight = jnp.sqrt(decay_rate)
    base_re, base_im = powers(decay_rate, pole_angle, offsets)
    taps = lax.optimization_barrier(jnp.sum(weight * (residue_real * base_re - residue_imag * base_im), axis=1))
    lag = jnp.arange(block_len)[:, None] - jnp.arange(block_len)[None, :]
    toeplitz = jnp.where((lag >= 0)[:, :, None], taps[jnp.clip(lag, 0, block_len - 1)], 0.0)
    next_re, next_im = powers(decay_rate, pole_angle, offsets + 1.0)
    out_re = weight * (residue_real * next_re - residue_imag * next_im)
    out_im = weight * (residue_real * next_im + residue_imag * next_re)
    in_re, in_im = powers(decay_rate, pole_angle, block_len - 1.0 - offsets)
    step_re, step_im = powers(decay_rate, pole_angle, jnp.float32(block_len))
    blocks = mixed.reshape(mixed.shape[0] // block_len, block_len, mixed.shape[1])

    def advance(carry, block):
        state_re, state_im = carry
        near = jnp.einsum('tsc,sc->tc', toeplitz, block, precision=highest)
        far = jnp.einsum('jmc,mc->jc', out_re, state_re, precision=highest) - jnp.einsum('jmc,mc->jc', out_im, state_im, precision=highest)
        enter_re = jnp.einsum('jmc,jc->mc', in_re, block, precision=highest)
        enter_im = jnp.einsum('jmc,jc->mc', in_im, block, precision=highest)
        new_re = step_re * state_re - step_im * state_im + enter_re
        new_im = step_re * state_im + step_im * state_re + enter_im
        return ((new_re, new_im), near + far)
    zeros = jnp.zeros_like(decay_rate)
    final_state, outputs = lax.scan(advance, (zeros, zeros), blocks)
    conv = outputs.reshape(mixed.shape)
    gated = query_proj.astype(jnp.float32) * (conv + skip_gain * mixed)
    power = lax.optimization_barrier(jnp.mean(gated * gated, axis=1, keepdims=True))
    return (gated * norm_gain * lax.rsqrt(power + 1e-05)).astype(jnp.bfloat16)
```

```python
import functools

import jax
import jax.numpy as jnp
from jax import lax
from jax.experimental import pallas as pl
from jax.experimental.pallas import tpu as pltpu
from jax.sharding import PartitionSpec as P

F32 = jnp.float32
SUB = 8
LANE = 128
BLOCK = 16
STEP = 256
VMEM_LIMIT = 48 * 2**20


def cmul(ar, ai, br, bi):
    return ar * br - ai * bi, ar * bi + ai * br


def cos_sin(r, n):
    z = r * r
    s = r + r * z * (-1.66666667e-1 + z * (8.33333310e-3 + z * (-1.98409296e-4 + z * 2.7181716e-6)))
    c = 1.0 + z * (-0.5 + z * (4.16666664e-2 + z * (-1.38888642e-3 + z * 2.4760495e-5)))
    quarter = n - 4.0 * jnp.floor(n * 0.25)
    odd = (quarter == 1.0) | (quarter == 3.0)
    sin = jnp.where(odd, c, s)
    cos = jnp.where(odd, s, c)
    sin = jnp.where(quarter >= 2.0, -sin, sin)
    cos = jnp.where((quarter == 1.0) | (quarter == 2.0), -cos, cos)
    return cos, sin


def pole_power(decay, angle, count):
    phase = angle * float(count)
    n = jnp.floor(phase * 0.6366197723675814 + 0.5)
    r = ((phase - n * 1.5703125) - n * 4.837512969970703125e-4) - n * 7.549789948768648e-8
    cos, sin = cos_sin(r, n)
    size = jnp.exp(decay * -float(count))
    return size * cos, size * sin


def power_table(pr, pi, first_r, first_i, count):
    tr, ti = [first_r], [first_i]
    for _ in range(count - 1):
        r, i = cmul(tr[-1], ti[-1], pr, pi)
        tr.append(r)
        ti.append(i)
    return tr, ti


def squared(r, i, times):
    for _ in range(times):
        r, i = r * r - i * i, (r + r) * i
    return r, i


def row(ref, index):
    return jnp.broadcast_to(ref[index : index + 1, :], (SUB, LANE))


def end_state_kernel(with_power, off_ref, k_ref, v_ref, a_ref, th_ref, rr_ref, ri_ref, *rest):
    if with_power:
        e_ref, l_ref, hp_ref, pw_ref, xs = rest
    else:
        e_ref, l_ref, hp_ref, xs = rest
    rows = k_ref.shape[0]
    modes = a_ref.shape[0]
    for g in range(k_ref.shape[1] // LANE):
        ls = slice(g * LANE, (g + 1) * LANE)
        xs[...] = k_ref[:, ls].astype(F32) * v_ref[:, ls].astype(F32)
        taps = None
        for m0 in range(0, modes, SUB):
            ms = slice(m0, m0 + SUB)
            decay, angle = a_ref[ms, ls], th_ref[ms, ls]
            pr, pi = pole_power(decay, angle, 1)
            weight = jnp.sqrt(decay)
            tr, ti = power_table(pr, pi, weight * rr_ref[ms, ls], weight * ri_ref[ms, ls], BLOCK)
            taps = tr if taps is None else [x + y for x, y in zip(taps, tr)]
            qr, qi = squared(pr, pi, BLOCK.bit_length() - 1)
            sr = jnp.zeros((SUB, LANE), F32)
            si = jnp.zeros((SUB, LANE), F32)
            for b in range(rows // BLOCK):
                at = b * 2 * modes + m0
                l_ref[at : at + SUB, ls] = sr
                l_ref[at + modes : at + modes + SUB, ls] = si
                sr, si = cmul(qr, qi, sr, si)
                for s in range(BLOCK):
                    x = row(xs, b * BLOCK + s)
                    sr = sr + tr[BLOCK - 1 - s] * x
                    si = si + ti[BLOCK - 1 - s] * x
            e_ref[ms, ls] = sr
            e_ref[modes + m0 : modes + m0 + SUB, ls] = si
            if with_power:
                wr, wi = pole_power(decay, angle, rows)
                pw_ref[ms, ls] = wr
                pw_ref[modes + m0 : modes + m0 + SUB, ls] = wi
        for j in range(BLOCK):
            hp_ref[j * SUB : (j + 1) * SUB, ls] = taps[j]


def near_kernel(off_ref, k_ref, v_ref, hp_ref, skip_ref, y_ref, xs):
    rows = k_ref.shape[0]
    blocks = rows // BLOCK
    for g in range(k_ref.shape[1] // LANE):
        ls = slice(g * LANE, (g + 1) * LANE)
        xs[...] = k_ref[:, ls].astype(F32) * v_ref[:, ls].astype(F32)
        taps = []
        for j in range(BLOCK):
            tap = jnp.sum(hp_ref[j * SUB : (j + 1) * SUB, ls], axis=0, keepdims=True)
            if j == 0:
                tap = tap + skip_ref[0:1, ls]
            taps.append(jnp.broadcast_to(tap, (SUB, LANE)))
        for a0 in range(0, blocks, SUB):
            acc = [None] * BLOCK
            for s in range(BLOCK):
                x = xs[pl.ds(a0 * BLOCK + s, SUB, stride=BLOCK), :]
                for t in range(s, BLOCK):
                    part = taps[t - s] * x
                    acc[t] = part if acc[t] is None else acc[t] + part
            for t in range(BLOCK):
                y_ref[t * blocks + a0 : t * blocks + a0 + SUB, ls] = acc[t]


def far_kernel(off_ref, s_ref, l_ref, y_ref, a_ref, th_ref, q_ref, gated_ref, power_ref, table, state, conv):
    rows = q_ref.shape[0]
    modes = a_ref.shape[0]
    blocks = rows // BLOCK

    @pl.when(pl.program_id(0) == 0)
    def _():
        power_ref[...] = jnp.zeros_like(power_ref)

    for g in range(q_ref.shape[1] // LANE):
        ls = slice(g * LANE, (g + 1) * LANE)
        for m0 in range(0, modes, SUB):
            ms = slice(m0, m0 + SUB)
            pr, pi = pole_power(a_ref[ms, ls], th_ref[ms, ls], 1)
            tr, ti = power_table(pr, pi, pr, pi, BLOCK)
            for j in range(BLOCK):
                at = j * 2 * modes + m0
                table[at : at + SUB, :] = tr[j]
                table[at + modes : at + modes + SUB, :] = ti[j]
            qr, qi = tr[-1], ti[-1]
            sr, si = s_ref[ms, ls], s_ref[modes + m0 : modes + m0 + SUB, ls]
            for b in range(blocks):
                at = b * 2 * modes + m0
                state[at : at + SUB, :] = l_ref[at : at + SUB, ls] + sr
                state[at + modes : at + modes + SUB, :] = l_ref[at + modes : at + modes + SUB, ls] + si
                if b < blocks - 1:
                    sr, si = cmul(qr, qi, sr, si)
        starts = range(0, blocks, SUB)
        acc = {
            (t, a0): y_ref[t * blocks + a0 : t * blocks + a0 + SUB, ls] for t in range(BLOCK) for a0 in starts
        }
        for m in range(modes):
            cr = {a0: state[pl.ds(a0 * 2 * modes + m, SUB, stride=2 * modes), :] for a0 in starts}
            ci = {a0: state[pl.ds(a0 * 2 * modes + modes + m, SUB, stride=2 * modes), :] for a0 in starts}
            for t in range(BLOCK):
                br = row(table, t * 2 * modes + m)
                bi = row(table, t * 2 * modes + modes + m)
                for a0 in starts:
                    acc[t, a0] = acc[t, a0] + cr[a0] * br - ci[a0] * bi
        for (t, a0), y in acc.items():
            conv[pl.ds(a0 * BLOCK + t, SUB, stride=BLOCK), :] = y
        gated = q_ref[:, ls].astype(F32) * conv[...]
        gated_ref[:, ls] = gated
        power_ref[...] += gated * gated


def norm_kernel(steps, off_ref, scale_ref, own_ref, other_ref, gain_ref, out_ref):
    step = pl.program_id(0)

    @pl.when(step < steps)
    def _():
        out_ref[...] = (own_ref[...] * gain_ref[...] * scale_ref[:, 0:1]).astype(out_ref.dtype)

    @pl.when(step >= steps)
    def _():
        out_ref[...] = (other_ref[...] * gain_ref[...] * scale_ref[:, 0:1]).astype(out_ref.dtype)


def call(kernel, offset, steps, ins, outs, scratch):
    def spec(rows, place):
        if place == "half":
            return pl.BlockSpec((rows, STEP), lambda i, off: (0, off[0] * steps + i))
        if place == "local":
            return pl.BlockSpec((rows, STEP), lambda i, off: (0, i))
        return pl.BlockSpec((rows, LANE), lambda i, off: (0, 0))

    return pl.pallas_call(
        kernel,
        grid_spec=pltpu.PrefetchScalarGridSpec(
            num_scalar_prefetch=1,
            grid=(steps,),
            in_specs=[spec(rows, place) for _, rows, place in ins],
            out_specs=[spec(rows, place) for _, _, rows, place in outs],
            scratch_shapes=scratch,
        ),
        out_shape=[jax.ShapeDtypeStruct(shape, dtype) for shape, dtype, _, _ in outs],
        compiler_params=pltpu.CompilerParams(vmem_limit_bytes=VMEM_LIMIT),
    )(offset, *[x for x, _, _ in ins])


def exchange(x, axis, distance):
    return lax.ppermute(x, axis, [(i, i ^ distance) for i in range(lax.axis_size(axis))])


def parts(x):
    half = x.shape[0] // 2
    return x[:half], x[half:]


def times(x, y):
    return jnp.concatenate(cmul(*parts(x), *parts(y)))


def per_device(q, k, v, decay, angle, res_r, res_i, skip_gain, norm_gain):
    rows, width = q.shape
    modes = decay.shape[0]
    half = width // 2
    steps = half // STEP
    blocks = rows // BLOCK
    count = lax.axis_size("seq")
    me = lax.axis_index("seq")
    upper = (me & 1) == 1
    own = (me & 1).astype(jnp.int32).reshape(1)
    other = 1 - own
    skip = skip_gain.reshape(1, width)
    gain = norm_gain.reshape(1, width)
    states = 2 * modes

    def end_state(offset, with_power):
        outs = [
            ((states, half), F32, states, "local"),
            ((blocks * states, half), F32, blocks * states, "local"),
            ((BLOCK * SUB, half), F32, BLOCK * SUB, "local"),
        ]
        if with_power:
            outs.append(((states, half), F32, states, "local"))
        ins = [(k, rows, "half"), (v, rows, "half")] + [
            (x, modes, "half") for x in (decay, angle, res_r, res_i)
        ]
        return call(
            functools.partial(end_state_kernel, with_power),
            offset, steps, ins, outs, [pltpu.VMEM((rows, LANE), F32)],
        )

    def near(offset, taps):
        ins = [(k, rows, "half"), (v, rows, "half"), (taps, BLOCK * SUB, "local"), (skip, 1, "half")]
        outs = [((rows, half), F32, rows, "local")]
        return call(near_kernel, offset, steps, ins, outs, [pltpu.VMEM((rows, LANE), F32)])[0]

    def far(offset, start, local, y):
        ins = [
            (start, states, "local"),
            (local, blocks * states, "local"),
            (y, rows, "local"),
            (decay, modes, "half"),
            (angle, modes, "half"),
            (q, rows, "half"),
        ]
        outs = [((rows, half), F32, rows, "local"), ((rows, LANE), F32, rows, "fixed")]
        scratch = [
            pltpu.VMEM((BLOCK * states, LANE), F32),
            pltpu.VMEM((blocks * states, LANE), F32),
            pltpu.VMEM((rows, LANE), F32),
        ]
        return call(far_kernel, offset, steps, ins, outs, scratch)

    sent_end, sent_local, sent_taps = end_state(other, False)
    pair_end = exchange(sent_end, "seq", 1)
    own_end, own_local, own_taps, step_power = end_state(own, True)
    own_near = near(own, own_taps)
    other_near = near(other, sent_taps)
    low = jnp.where(upper, pair_end, own_end)
    high = jnp.where(upper, own_end, pair_end)
    total = times(step_power, low) + high
    before = jnp.zeros_like(total)
    jump = times(step_power, step_power)
    mine = jnp.concatenate([jnp.ones((modes, half), F32), jnp.zeros((modes, half), F32)])
    distance = 2
    while distance < count:
        got = exchange(total, "seq", distance)
        above = (me & distance) != 0
        before = jnp.where(above, before + times(mine, got), before)
        total = jnp.where(above, times(jump, got) + total, times(jump, total) + got)
        mine = jnp.where(above, times(mine, jump), mine)
        jump = times(jump, jump)
        distance *= 2
    after_low = times(step_power, before) + low
    own_start = jnp.where(upper, after_low, before)
    other_start = exchange(jnp.where(upper, before, after_low), "seq", 1)
    own_gated, own_power = far(own, own_start, own_local, own_near)
    other_gated, other_power = far(other, other_start, sent_local, other_near)
    power = jnp.sum(own_power + other_power, axis=1)
    distance = 1
    while distance < lax.axis_size("ch"):
        power = power + exchange(power, "ch", distance)
        distance *= 2
    scale = lax.rsqrt(power / (width * lax.axis_size("ch")) + 1e-05)
    scale = jnp.broadcast_to(scale[:, None], (rows, LANE))

    def place(i, off):
        return (0, lax.rem(off[0] * steps + i, 2 * steps))

    return pl.pallas_call(
        functools.partial(norm_kernel, steps),
        grid_spec=pltpu.PrefetchScalarGridSpec(
            num_scalar_prefetch=1,
            grid=(2 * steps,),
            in_specs=[
                pl.BlockSpec((rows, LANE), lambda i, off: (0, 0)),
                pl.BlockSpec((rows, STEP), lambda i, off: (0, jnp.minimum(i, steps - 1))),
                pl.BlockSpec((rows, STEP), lambda i, off: (0, jnp.maximum(i - steps, 0))),
                pl.BlockSpec((1, STEP), place),
            ],
            out_specs=pl.BlockSpec((rows, STEP), place),
        ),
        out_shape=jax.ShapeDtypeStruct((rows, width), jnp.bfloat16),
        compiler_params=pltpu.CompilerParams(vmem_limit_bytes=VMEM_LIMIT),
    )(own, scale, own_gated, other_gated, gain)


def solution(mesh):
    rows = P("seq", "ch")
    poles = P(None, "ch")
    return jax.shard_map(
        per_device,
        mesh=mesh,
        in_specs=(rows, rows, rows, poles, poles, poles, poles, P("ch"), P("ch")),
        out_specs=rows,
        check_vma=False,
    )
```

```python
import functools

import jax
import jax.numpy as jnp
from jax import lax
from jax.experimental import pallas as pl
from jax.experimental.pallas import tpu as pltpu
from jax.sharding import PartitionSpec as P

F32 = jnp.float32
SUB = 8
LANE = 128
BLOCK = 16
APART = BLOCK + 1
FETCH = 256
STORE = 512
TAIL = 2
TOKENS = 8
VMEM_LIMIT = 8 * 2**20


def cmul(ar, ai, br, bi):
    return ar * br - ai * bi, ar * bi + ai * br


def cos_sin(r, n):
    z = r * r
    s = r + r * z * (-1.66666667e-1 + z * (8.33333310e-3 + z * (-1.98409296e-4 + z * 2.7181716e-6)))
    c = 1.0 + z * (-0.5 + z * (4.16666664e-2 + z * (-1.38888642e-3 + z * 2.4760495e-5)))
    quarter = n - 4.0 * jnp.floor(n * 0.25)
    odd = (quarter == 1.0) | (quarter == 3.0)
    sin = jnp.where(odd, c, s)
    cos = jnp.where(odd, s, c)
    sin = jnp.where(quarter >= 2.0, -sin, sin)
    cos = jnp.where((quarter == 1.0) | (quarter == 2.0), -cos, cos)
    return cos, sin


def pole_power(decay, angle, count):
    phase = angle * float(count)
    n = jnp.floor(phase * 0.6366197723675814 + 0.5)
    r = ((phase - n * 1.5703125) - n * 4.837512969970703125e-4) - n * 7.549789948768648e-8
    cos, sin = cos_sin(r, n)
    size = jnp.exp(decay * -float(count))
    return size * cos, size * sin


def power_table(pr, pi, first_r, first_i, count):
    tr, ti = [first_r], [first_i]
    for _ in range(count - 1):
        r, i = cmul(tr[-1], ti[-1], pr, pi)
        tr.append(r)
        ti.append(i)
    return tr, ti


def squared(r, i, times):
    for _ in range(times):
        r, i = r * r - i * i, (r + r) * i
    return r, i


def lanes(start, group):
    return pl.ds(pl.multiple_of(start + group * LANE, LANE), LANE)


def row(ref, index, ls):
    return jnp.broadcast_to(ref[index : index + 1, ls], (SUB, LANE))


def pole_table(a_ref, th_ref, rr_ref, ri_ref, ms, src):
    decay, angle = a_ref[ms, src], th_ref[ms, src]
    pr, pi = pole_power(decay, angle, 1)
    weight = jnp.sqrt(decay)
    return pr, pi, power_table(pr, pi, weight * rr_ref[ms, src], weight * ri_ref[ms, src], BLOCK)


def stream(groups, stores, body):
    def copies(g):
        return [pltpu.make_async_copy(buf.at[g], out.at[g], sem.at[g]) for buf, out, sem in stores]

    def fill(g, carry):
        body(g)
        for copy in copies(g):
            copy.start()
        return carry

    def finish(g, carry):
        for copy in copies(g):
            copy.wait()
        return carry

    lax.fori_loop(0, groups, fill, 0)
    return lambda: lax.fori_loop(0, groups, finish, 0)


def rest(start, stop, body):
    def step(g, carry):
        body(g)
        return carry

    lax.fori_loop(start, stop, step, 0)


def end_states(mixed, poles, at, e_ref, l_buf, pw_ref=None):
    a_ref, th_ref = poles[:2]
    rows = mixed.shape[0]
    modes = a_ref.shape[0]
    src, dst = at
    every = slice(None)
    for m0 in range(0, modes, SUB):
        ms = slice(m0, m0 + SUB)
        pr, pi, (tr, ti) = pole_table(*poles, ms, src)
        qr, qi = squared(pr, pi, BLOCK.bit_length() - 1)
        sr = jnp.zeros((SUB, LANE), F32)
        si = jnp.zeros((SUB, LANE), F32)
        for b in range(rows // BLOCK):
            base = b * 2 * modes + m0
            if l_buf is not None:
                l_buf[base : base + SUB, :] = sr
                l_buf[base + modes : base + modes + SUB, :] = si
            sr, si = cmul(qr, qi, sr, si)
            for s in range(BLOCK):
                x = row(mixed, b * BLOCK + s, every)
                sr = sr + tr[BLOCK - 1 - s] * x
                si = si + ti[BLOCK - 1 - s] * x
        if e_ref is not None:
            e_ref[ms, dst] = sr
            e_ref[modes + m0 : modes + m0 + SUB, dst] = si
        if pw_ref is not None:
            wr, wi = pole_power(a_ref[ms, src], th_ref[ms, src], rows)
            pw_ref[ms, dst] = wr
            pw_ref[modes + m0 : modes + m0 + SUB, dst] = wi


def sent_kernel(off_ref, k_hbm, v_hbm, a_hbm, th_hbm, rr_hbm, ri_hbm, e_ref, l_hbm, kb, vb, pb, mixed, l_buf, kv_sem, p_sem, l_sem):
    half = e_ref.shape[1]
    chunks = half // FETCH
    base = off_ref[0] * half

    def there(c):
        return pl.ds(pl.multiple_of(base + c * FETCH, LANE), FETCH)

    def here(c):
        return pl.ds(pl.multiple_of(c * FETCH, LANE), FETCH)

    def fetches(c):
        return [
            pltpu.make_async_copy(src.at[:, there(c)], dst.at[:, here(c)], kv_sem.at[i, c])
            for i, (src, dst) in enumerate(((k_hbm, kb), (v_hbm, vb)))
        ]

    whole = pl.ds(pl.multiple_of(base, LANE), half)
    poles = [
        pltpu.make_async_copy(src.at[:, whole], pb.at[i], p_sem.at[i])
        for i, src in enumerate((a_hbm, th_hbm, rr_hbm, ri_hbm))
    ]
    for copy in fetches(0) + poles:
        copy.start()
    for c in range(1, chunks):
        for copy in fetches(c):
            copy.start()
    for copy in poles:
        copy.wait()

    def group(g, l_buf):
        @pl.when(lax.rem(g, FETCH // LANE) == 0)
        def _():
            for copy in fetches(g // (FETCH // LANE)):
                copy.wait()

        ls = lanes(0, g)
        mixed[...] = kb[:, ls].astype(F32) * vb[:, ls].astype(F32)
        end_states(mixed, [pb.at[i] for i in range(4)], (ls, ls), e_ref, l_buf)

    stored = l_hbm.shape[0]
    finish = stream(stored, [(l_buf, l_hbm, l_sem)], lambda g: group(g, l_buf.at[g]))
    rest(stored, half // LANE, lambda g: group(g, None))
    finish()


def own_kernel(off_ref, k_ref, v_ref, a_ref, th_ref, rr_ref, ri_ref, e_ref, pw_ref, l_hbm, mixed, l_buf, l_sem):
    half = e_ref.shape[1]

    def group(g, l_buf):
        src, dst = lanes(off_ref[0] * half, g), lanes(0, g)
        mixed[...] = k_ref[:, src].astype(F32) * v_ref[:, src].astype(F32)
        end_states(mixed, (a_ref, th_ref, rr_ref, ri_ref), (src, dst), e_ref, l_buf, pw_ref)

    stored = l_hbm.shape[0]
    finish = stream(stored, [(l_buf, l_hbm, l_sem)], lambda g: group(g, l_buf.at[g]))
    rest(stored, half // LANE, lambda g: group(g, None))
    finish()


def fill_table(table, pr, pi, m0, modes):
    tr, ti = power_table(pr, pi, pr, pi, BLOCK)
    for j in range(BLOCK):
        base = j * 2 * modes + m0
        table[base : base + SUB, :] = tr[j]
        table[base + modes : base + modes + SUB, :] = ti[j]


def near_kernel(
    off_ref, after_ref, k_ref, v_ref, a_ref, th_ref, rr_ref, ri_ref, skip_ref, *refs
):
    with_table = len(refs) > 8
    if with_table:
        l_hbm, y_hbm, table_hbm, plain, mixed, l_buf, y_buf, l_sem, y_sem, table_buf, table_sem = refs
    else:
        l_hbm, y_hbm, plain, mixed, l_buf, y_buf, l_sem, y_sem = refs
    rows = k_ref.shape[0]
    modes = a_ref.shape[0]
    groups = y_hbm.shape[0]
    half = groups * LANE
    blocks = rows // BLOCK

    def group(g):
        src = lanes(off_ref[0] * half, g)
        for b in range(blocks):
            bs = slice(b * BLOCK, (b + 1) * BLOCK)
            mixed[b * APART : b * APART + BLOCK, :] = k_ref[bs, src].astype(F32) * v_ref[bs, src].astype(F32)
        sums = None
        for m0 in range(0, modes, SUB):
            pr, pi, (tr, _) = pole_table(a_ref, th_ref, rr_ref, ri_ref, slice(m0, m0 + SUB), src)
            sums = tr if sums is None else [x + y for x, y in zip(sums, tr)]
            if with_table:
                fill_table(table_buf.at[g], pr, pi, m0, modes)
        taps = []
        for j in range(BLOCK):
            tap = jnp.sum(sums[j], axis=0, keepdims=True)
            if j == 0:
                tap = tap + skip_ref[0:1, src]
            taps.append(jnp.broadcast_to(tap, (SUB, LANE)))
        for a0 in range(0, blocks, SUB):
            acc = [None] * BLOCK
            for s in range(BLOCK):
                x = mixed[pl.ds(a0 * APART + s, SUB, stride=APART), :]
                for t in range(s, BLOCK):
                    part = taps[t - s] * x
                    acc[t] = part if acc[t] is None else acc[t] + part
            for t in range(BLOCK):
                y_buf[g, t * blocks + a0 : t * blocks + a0 + SUB, :] = acc[t]

    tail = l_hbm.shape[0]

    def states(i):
        src = lanes(off_ref[0] * half, groups - tail + i)
        plain[...] = k_ref[:, src].astype(F32) * v_ref[:, src].astype(F32)
        end_states(plain, (a_ref, th_ref, rr_ref, ri_ref), (src, src), None, l_buf.at[i])

    finish_states = stream(tail, [(l_buf, l_hbm, l_sem)], states)
    stores = [(y_buf, y_hbm, y_sem)] + ([(table_buf, table_hbm, table_sem)] if with_table else [])
    finish = stream(groups, stores, group)
    finish_states()
    finish()


def far_kernel(with_table, off_ref, s_ref, l_ref, tail_ref, y_ref, q_ref, *refs):
    if with_table:
        table_ref, gated_ref, power_ref, state, conv = refs
    else:
        a_ref, th_ref, gated_ref, power_ref, state, conv, own_table = refs
    rows = q_ref.shape[0]
    modes = s_ref.shape[0] // 2
    groups = y_ref.shape[0]
    half = groups * LANE
    blocks = rows // BLOCK
    starts = range(0, blocks, SUB)
    apart = 2 * modes + 1
    every = slice(None)
    power_ref[...] = jnp.zeros_like(power_ref)

    def group(g, l_ref):
        src, dst = lanes(off_ref[0] * half, g), lanes(0, g)
        table = table_ref.at[g] if with_table else own_table
        for m0 in range(0, modes, SUB):
            ms = slice(m0, m0 + SUB)
            if not with_table:
                fill_table(table, *pole_power(a_ref[ms, src], th_ref[ms, src], 1), m0, modes)
            last = (BLOCK - 1) * 2 * modes + m0
            qr, qi = table[last : last + SUB, :], table[last + modes : last + modes + SUB, :]
            sr, si = s_ref[ms, dst], s_ref[modes + m0 : modes + m0 + SUB, dst]
            for b in range(blocks):
                at = b * 2 * modes + m0
                to = b * apart + m0
                state[to : to + SUB, :] = l_ref[at : at + SUB, :] + sr
                state[to + modes : to + modes + SUB, :] = l_ref[at + modes : at + modes + SUB, :] + si
                if b < blocks - 1:
                    sr, si = cmul(qr, qi, sr, si)
        for t0 in range(0, BLOCK, TOKENS):
            acc = {
                (t, a0): y_ref[g, t * blocks + a0 : t * blocks + a0 + SUB, :]
                for t in range(t0, t0 + TOKENS)
                for a0 in starts
            }
            for m in range(modes):
                cr = {a0: state[pl.ds(a0 * apart + m, SUB, stride=apart), :] for a0 in starts}
                ci = {a0: state[pl.ds(a0 * apart + modes + m, SUB, stride=apart), :] for a0 in starts}
                for t in range(t0, t0 + TOKENS):
                    br = row(table, t * 2 * modes + m, every)
                    bi = row(table, t * 2 * modes + modes + m, every)
                    for a0 in starts:
                        acc[t, a0] = acc[t, a0] + cr[a0] * br - ci[a0] * bi
            for (t, a0), y in acc.items():
                conv[pl.ds(a0 * APART + t, SUB, stride=APART), :] = y
        for b in range(blocks):
            bs = slice(b * BLOCK, (b + 1) * BLOCK)
            gated = q_ref[bs, src].astype(F32) * conv[b * APART : b * APART + BLOCK, :]
            gated_ref[bs, dst] = gated
            power_ref[bs, :] += gated * gated

    stored = l_ref.shape[0]
    rest(0, stored, lambda g: group(g, l_ref.at[g]))
    rest(stored, groups, lambda g: group(g, tail_ref.at[g - stored]))


def norm_kernel(off_ref, own_ref, other_ref, scale_ref, gain_ref, out_hbm, buf, sem):
    half = own_ref.shape[1]
    copies = []
    for ref, base in ((own_ref, off_ref[0] * half), (other_ref, (1 - off_ref[0]) * half)):
        for first in range(0, half, STORE):
            at = len(copies) * STORE
            for g in range(STORE // LANE):
                gain = gain_ref[0:1, lanes(base + first, g)]
                gated = ref[:, first + g * LANE : first + (g + 1) * LANE]
                buf[:, at + g * LANE : at + (g + 1) * LANE] = (gated * gain * scale_ref[...]).astype(buf.dtype)
            to = pl.ds(pl.multiple_of(base + first, LANE), STORE)
            copies.append(pltpu.make_async_copy(buf.at[:, at : at + STORE], out_hbm.at[:, to], sem.at[len(copies)]))
            copies[-1].start()
    for copy in copies:
        copy.wait()


def call(kernel, offset, ins, outs, far_outs, scratch, space=pltpu.VMEM, dtype=F32):
    return pl.pallas_call(
        kernel,
        in_specs=[pl.BlockSpec(memory_space=pltpu.SMEM)] + [pl.BlockSpec(memory_space=space)] * len(ins),
        out_specs=[pl.BlockSpec(memory_space=pltpu.VMEM)] * len(outs)
        + [pl.BlockSpec(memory_space=pltpu.HBM)] * len(far_outs),
        out_shape=[pltpu.VMEM(shape, dtype) for shape in outs] + [pltpu.HBM(shape, dtype) for shape in far_outs],
        scratch_shapes=scratch,
        compiler_params=pltpu.CompilerParams(vmem_limit_bytes=VMEM_LIMIT),
    )(offset, *[pltpu.with_memory_space_constraint(x, space) for x in ins])


def exchange(x, axis, distance):
    return lax.ppermute(x, axis, [(i, i ^ distance) for i in range(lax.axis_size(axis))])


def parts(x):
    half = x.shape[0] // 2
    return x[:half], x[half:]


def times(x, y):
    return jnp.concatenate(cmul(*parts(x), *parts(y)))


def per_device(q, k, v, decay, angle, res_r, res_i, skip_gain, norm_gain):
    rows, width = q.shape
    modes = decay.shape[0]
    half = width // 2
    blocks = rows // BLOCK
    count = lax.axis_size("seq")
    me = lax.axis_index("seq")
    upper = (me & 1) == 1
    own = (me & 1).astype(jnp.int32).reshape(1)
    other = 1 - own
    skip = skip_gain.reshape(1, width)
    gain = norm_gain.reshape(1, width)
    states = 2 * modes
    poles = (decay, angle, res_r, res_i)
    mixed = pltpu.VMEM((rows, LANE), F32)
    padded = pltpu.VMEM((blocks * APART, LANE), F32)
    state = (states, half)
    groups = half // LANE
    local = (groups - TAIL, blocks * states, LANE)
    tail = (TAIL, blocks * states, LANE)
    table = (groups, BLOCK * states, LANE)
    near_shape = (groups, rows, LANE)

    group_sem = pltpu.SemaphoreType.DMA((groups,))
    stored_sem = pltpu.SemaphoreType.DMA((groups - TAIL,))

    def near(offset, after, with_table):
        ins = [after, k, v, *poles, skip]
        outs = [tail, near_shape]
        tail_sem = pltpu.SemaphoreType.DMA((TAIL,))
        scratch = [mixed, padded, pltpu.VMEM(tail, F32), pltpu.VMEM(near_shape, F32), tail_sem, group_sem]
        if with_table:
            outs.append(table)
            scratch += [pltpu.VMEM(table, F32), group_sem]
        return call(near_kernel, offset, ins, [], outs, scratch)

    def far(offset, start, local, tail, y, *table):
        ins = [start, local, tail, y, q, *(table or (decay, angle))]
        scratch = [pltpu.VMEM((blocks * (states + 1), LANE), F32), padded]
        if not table:
            scratch.append(pltpu.VMEM((BLOCK * states, LANE), F32))
        kernel = functools.partial(far_kernel, bool(table))
        return call(kernel, offset, ins, [(rows, half), (rows, LANE)], [], scratch)

    scratch = [
        pltpu.VMEM((rows, half), k.dtype),
        pltpu.VMEM((rows, half), v.dtype),
        pltpu.VMEM((4, modes, half), F32),
        mixed,
        pltpu.VMEM(local, F32),
        pltpu.SemaphoreType.DMA((2, half // FETCH)),
        pltpu.SemaphoreType.DMA((4,)),
        stored_sem,
    ]
    sent_end, sent_local = call(sent_kernel, other, [k, v, *poles], [state], [local], scratch, pltpu.HBM)
    pair_end = exchange(sent_end, "seq", 1)
    scratch = [mixed, pltpu.VMEM(local, F32), stored_sem]
    own_end, step_power, own_local = call(own_kernel, own, [k, v, *poles], [state] * 2, [local], scratch)
    low = jnp.where(upper, pair_end, own_end)
    high = jnp.where(upper, own_end, pair_end)
    total = times(step_power, low) + high
    before = mine = None
    jump = times(step_power, step_power)
    pending = [own, other]
    ready = []
    distance = 2
    while distance < count:
        got = exchange(total, "seq", distance)
        if pending:
            ready.append(near(pending.pop(0), total, False))
            got, ready[-1] = lax.optimization_barrier((got, ready[-1]))
        above = (me & distance) != 0
        if before is None:
            before = jnp.where(above, got, 0.0)
            mine = jnp.concatenate([jnp.where(above, parts(jump)[0], 1.0), jnp.where(above, parts(jump)[1], 0.0)])
        else:
            before = jnp.where(above, before + times(mine, got), before)
            mine = jnp.where(above, times(mine, jump), mine)
        total = jnp.where(above, times(jump, got) + total, times(jump, total) + got)
        jump = times(jump, jump)
        distance *= 2
    for offset in pending:
        ready.append(near(offset, total, False))
    after_low = times(step_power, before) + low
    own_start = jnp.where(upper, after_low, before)
    other_start = exchange(jnp.where(upper, before, after_low), "seq", 1)
    own_gated, own_power = far(own, own_start, own_local, *ready[0])
    other_gated, other_power = far(other, other_start, sent_local, *ready[1])
    power = jnp.sum(own_power + other_power, axis=1)
    distance = 1
    while distance < lax.axis_size("ch"):
        power = power + exchange(power, "ch", distance)
        distance *= 2
    scale = lax.rsqrt(power / (width * lax.axis_size("ch")) + 1e-05)
    scale = jnp.broadcast_to(scale[:, None], (rows, LANE))
    scratch = [pltpu.VMEM((rows, width), jnp.bfloat16), pltpu.SemaphoreType.DMA((width // STORE,))]
    ins = [own_gated, other_gated, scale, gain]
    return call(norm_kernel, own, ins, [], [(rows, width)], scratch, dtype=jnp.bfloat16)[0]


def solution(mesh):
    rows = P("seq", "ch")
    poles = P(None, "ch")
    return jax.shard_map(
        per_device,
        mesh=mesh,
        in_specs=(rows, rows, rows, poles, poles, poles, poles, P("ch"), P("ch")),
        out_specs=rows,
        check_vma=False,
    )
```

```python
import functools

import jax
import jax.numpy as jnp
from jax import lax
from jax.experimental import pallas as pl
from jax.experimental.pallas import tpu as pltpu
from jax.sharding import PartitionSpec as P

F32 = jnp.float32
SUB = 8
LANE = 128
BLOCK = 16
APART = BLOCK + 1
FETCH = 256
STORE = 512
TAIL = 2
TOKENS = 8
VMEM_LIMIT = 8 * 2**20


def cmul(ar, ai, br, bi):
    return ar * br - ai * bi, ar * bi + ai * br


def cos_sin(r, n):
    z = r * r
    s = r + r * z * (-1.66666667e-1 + z * (8.33333310e-3 + z * (-1.98409296e-4 + z * 2.7181716e-6)))
    c = 1.0 + z * (-0.5 + z * (4.16666664e-2 + z * (-1.38888642e-3 + z * 2.4760495e-5)))
    quarter = n - 4.0 * jnp.floor(n * 0.25)
    odd = (quarter == 1.0) | (quarter == 3.0)
    sin = jnp.where(odd, c, s)
    cos = jnp.where(odd, s, c)
    sin = jnp.where(quarter >= 2.0, -sin, sin)
    cos = jnp.where((quarter == 1.0) | (quarter == 2.0), -cos, cos)
    return cos, sin


def pole_power(decay, angle, count):
    phase = angle * float(count)
    n = jnp.floor(phase * 0.6366197723675814 + 0.5)
    r = ((phase - n * 1.5703125) - n * 4.837512969970703125e-4) - n * 7.549789948768648e-8
    cos, sin = cos_sin(r, n)
    size = jnp.exp(decay * -float(count))
    return size * cos, size * sin


def power_table(pr, pi, first_r, first_i, count):
    tr, ti = [first_r], [first_i]
    for _ in range(count - 1):
        r, i = cmul(tr[-1], ti[-1], pr, pi)
        tr.append(r)
        ti.append(i)
    return tr, ti


def squared(r, i, times):
    for _ in range(times):
        r, i = r * r - i * i, (r + r) * i
    return r, i


def lanes(start, group):
    return pl.ds(pl.multiple_of(start + group * LANE, LANE), LANE)


def row(ref, index, ls):
    return jnp.broadcast_to(ref[index : index + 1, ls], (SUB, LANE))


def pole_table(a_ref, th_ref, rr_ref, ri_ref, ms, src):
    decay, angle = a_ref[ms, src], th_ref[ms, src]
    pr, pi = pole_power(decay, angle, 1)
    weight = jnp.sqrt(decay)
    return pr, pi, power_table(pr, pi, weight * rr_ref[ms, src], weight * ri_ref[ms, src], BLOCK)


def stream(groups, stores, body):
    def copies(g):
        return [pltpu.make_async_copy(buf.at[g], out.at[g], sem.at[g]) for buf, out, sem in stores]

    def fill(g, carry):
        body(g)
        for copy in copies(g):
            copy.start()
        return carry

    def finish(g, carry):
        for copy in copies(g):
            copy.wait()
        return carry

    lax.fori_loop(0, groups, fill, 0)
    return lambda: lax.fori_loop(0, groups, finish, 0)


def rest(start, stop, body):
    def step(g, carry):
        body(g)
        return carry

    lax.fori_loop(start, stop, step, 0)


def end_states(mixed, poles, at, e_ref, l_buf, pw_ref=None):
    a_ref, th_ref = poles[:2]
    rows = mixed.shape[0]
    modes = a_ref.shape[0]
    src, dst = at
    every = slice(None)
    starts = range(0, modes, SUB)
    tables, jump, state = {}, {}, {}
    for m0 in starts:
        ms = slice(m0, m0 + SUB)
        pr, pi, tables[m0] = pole_table(*poles, ms, src)
        jump[m0] = squared(pr, pi, BLOCK.bit_length() - 1)
        state[m0] = jnp.zeros((SUB, LANE), F32), jnp.zeros((SUB, LANE), F32)
        if pw_ref is not None:
            wr, wi = pole_power(a_ref[ms, src], th_ref[ms, src], rows)
            pw_ref[ms, dst] = wr
            pw_ref[modes + m0 : modes + m0 + SUB, dst] = wi
    for b in range(rows // BLOCK):
        enter = {}
        for s in range(BLOCK):
            x = row(mixed, b * BLOCK + s, every)
            for m0 in starts:
                r, i = tables[m0][0][BLOCK - 1 - s] * x, tables[m0][1][BLOCK - 1 - s] * x
                enter[m0] = (r, i) if s == 0 else (enter[m0][0] + r, enter[m0][1] + i)
        for m0 in starts:
            base = b * 2 * modes + m0
            sr, si = state[m0]
            if l_buf is not None:
                l_buf[base : base + SUB, :] = sr
                l_buf[base + modes : base + modes + SUB, :] = si
            sr, si = cmul(*jump[m0], sr, si)
            state[m0] = sr + enter[m0][0], si + enter[m0][1]
    if e_ref is not None:
        for m0 in starts:
            e_ref[m0 : m0 + SUB, dst], e_ref[modes + m0 : modes + m0 + SUB, dst] = state[m0]


def sent_kernel(off_ref, k_hbm, v_hbm, a_hbm, th_hbm, rr_hbm, ri_hbm, e_ref, l_hbm, kb, vb, pb, mixed, l_buf, kv_sem, p_sem, l_sem):
    half = e_ref.shape[1]
    chunks = half // FETCH
    base = off_ref[0] * half

    def there(c):
        return pl.ds(pl.multiple_of(base + c * FETCH, LANE), FETCH)

    def here(c):
        return pl.ds(pl.multiple_of(c * FETCH, LANE), FETCH)

    def fetches(c):
        return [
            pltpu.make_async_copy(src.at[:, there(c)], dst.at[:, here(c)], kv_sem.at[i, c])
            for i, (src, dst) in enumerate(((k_hbm, kb), (v_hbm, vb)))
        ]

    whole = pl.ds(pl.multiple_of(base, LANE), half)
    poles = [
        pltpu.make_async_copy(src.at[:, whole], pb.at[i], p_sem.at[i])
        for i, src in enumerate((a_hbm, th_hbm, rr_hbm, ri_hbm))
    ]
    for copy in poles + fetches(0) + fetches(1):
        copy.start()
    for copy in poles:
        copy.wait()

    def group(g, l_buf):
        @pl.when(lax.rem(g, FETCH // LANE) == 0)
        def _():
            c = g // (FETCH // LANE)
            for copy in fetches(c):
                copy.wait()

            @pl.when(c + 2 < chunks)
            def _():
                for copy in fetches(c + 2):
                    copy.start()

        ls = lanes(0, g)
        mixed[...] = kb[:, ls].astype(F32) * vb[:, ls].astype(F32)
        end_states(mixed, [pb.at[i] for i in range(4)], (ls, ls), e_ref, l_buf)

    stored = l_hbm.shape[0]
    finish = stream(stored, [(l_buf, l_hbm, l_sem)], lambda g: group(g, l_buf.at[g]))
    rest(stored, half // LANE, lambda g: group(g, None))
    finish()


def own_kernel(off_ref, k_ref, v_ref, a_ref, th_ref, rr_ref, ri_ref, e_ref, pw_ref, l_hbm, mixed, l_buf, l_sem):
    half = e_ref.shape[1]

    def group(g, l_buf):
        src, dst = lanes(off_ref[0] * half, g), lanes(0, g)
        mixed[...] = k_ref[:, src].astype(F32) * v_ref[:, src].astype(F32)
        end_states(mixed, (a_ref, th_ref, rr_ref, ri_ref), (src, dst), e_ref, l_buf, pw_ref)

    stored = l_hbm.shape[0]
    finish = stream(stored, [(l_buf, l_hbm, l_sem)], lambda g: group(g, l_buf.at[g]))
    rest(stored, half // LANE, lambda g: group(g, None))
    finish()


def fill_table(table, pr, pi, m0, modes):
    tr, ti = power_table(pr, pi, pr, pi, BLOCK)
    for j in range(BLOCK):
        base = j * 2 * modes + m0
        table[base : base + SUB, :] = tr[j]
        table[base + modes : base + modes + SUB, :] = ti[j]


def near_kernel(
    off_ref, after_ref, k_ref, v_ref, a_ref, th_ref, rr_ref, ri_ref, skip_ref, *refs
):
    if len(refs) > 8:
        table_ref, *refs = refs
    else:
        table_ref = None
    l_hbm, y_hbm, plain, mixed, l_buf, y_buf, l_sem, y_sem = refs
    rows = k_ref.shape[0]
    modes = a_ref.shape[0]
    groups = y_hbm.shape[0]
    half = groups * LANE
    blocks = rows // BLOCK

    def group(g):
        src = lanes(off_ref[0] * half, g)
        for b in range(blocks):
            bs = slice(b * BLOCK, (b + 1) * BLOCK)
            mixed[b * APART : b * APART + BLOCK, :] = k_ref[bs, src].astype(F32) * v_ref[bs, src].astype(F32)
        sums = None
        for m0 in range(0, modes, SUB):
            pr, pi, (tr, _) = pole_table(a_ref, th_ref, rr_ref, ri_ref, slice(m0, m0 + SUB), src)
            sums = tr if sums is None else [x + y for x, y in zip(sums, tr)]
            if table_ref is not None:
                ms, there = slice(m0, m0 + SUB), lanes((1 - off_ref[0]) * half, g)
                fill_table(table_ref.at[g], *pole_power(a_ref[ms, there], th_ref[ms, there], 1), m0, modes)
        taps = []
        for j in range(BLOCK):
            tap = jnp.sum(sums[j], axis=0, keepdims=True)
            if j == 0:
                tap = tap + skip_ref[0:1, src]
            taps.append(jnp.broadcast_to(tap, (SUB, LANE)))
        for a0 in range(0, blocks, SUB):
            acc = [None] * BLOCK
            for s in range(BLOCK):
                x = mixed[pl.ds(a0 * APART + s, SUB, stride=APART), :]
                for t in range(s, BLOCK):
                    part = taps[t - s] * x
                    acc[t] = part if acc[t] is None else acc[t] + part
            for t in range(BLOCK):
                y_buf[g, t * blocks + a0 : t * blocks + a0 + SUB, :] = acc[t]

    tail = l_hbm.shape[0]

    def states(i):
        src = lanes(off_ref[0] * half, groups - tail + i)
        plain[...] = k_ref[:, src].astype(F32) * v_ref[:, src].astype(F32)
        end_states(plain, (a_ref, th_ref, rr_ref, ri_ref), (src, src), None, l_buf.at[i])

    finish_states = stream(tail, [(l_buf, l_hbm, l_sem)], states)
    finish = stream(groups, [(y_buf, y_hbm, y_sem)], group)
    finish_states()
    finish()


def far_kernel(off_ref, s_ref, l_ref, tail_ref, y_ref, q_ref, table_ref, *refs):
    if len(refs) > 4:
        a_ref, th_ref, gated_ref, power_ref, next_ref, state, conv = refs
    else:
        gated_ref, power_ref, state, conv = refs
        next_ref = None
    rows = q_ref.shape[0]
    modes = s_ref.shape[0] // 2
    groups = y_ref.shape[0]
    half = groups * LANE
    blocks = rows // BLOCK
    starts = range(0, blocks, SUB)
    apart = 2 * modes + 1
    every = slice(None)
    power_ref[...] = jnp.zeros_like(power_ref)

    def group(g, l_ref):
        src, dst = lanes(off_ref[0] * half, g), lanes(0, g)
        table = table_ref.at[g]
        for m0 in range(0, modes, SUB):
            ms = slice(m0, m0 + SUB)
            if next_ref is not None:
                there = lanes((1 - off_ref[0]) * half, g)
                fill_table(next_ref.at[g], *pole_power(a_ref[ms, there], th_ref[ms, there], 1), m0, modes)
            last = (BLOCK - 1) * 2 * modes + m0
            qr, qi = table[last : last + SUB, :], table[last + modes : last + modes + SUB, :]
            sr, si = s_ref[ms, dst], s_ref[modes + m0 : modes + m0 + SUB, dst]
            for b in range(blocks):
                at = b * 2 * modes + m0
                to = b * apart + m0
                state[to : to + SUB, :] = l_ref[at : at + SUB, :] + sr
                state[to + modes : to + modes + SUB, :] = l_ref[at + modes : at + modes + SUB, :] + si
                if b < blocks - 1:
                    sr, si = cmul(qr, qi, sr, si)
        for t0 in range(0, BLOCK, TOKENS):
            acc = {
                (t, a0): y_ref[g, t * blocks + a0 : t * blocks + a0 + SUB, :]
                for t in range(t0, t0 + TOKENS)
                for a0 in starts
            }
            for m in range(modes):
                cr = {a0: state[pl.ds(a0 * apart + m, SUB, stride=apart), :] for a0 in starts}
                ci = {a0: state[pl.ds(a0 * apart + modes + m, SUB, stride=apart), :] for a0 in starts}
                for t in range(t0, t0 + TOKENS):
                    br = row(table, t * 2 * modes + m, every)
                    bi = row(table, t * 2 * modes + modes + m, every)
                    for a0 in starts:
                        acc[t, a0] = acc[t, a0] + cr[a0] * br - ci[a0] * bi
            for (t, a0), y in acc.items():
                conv[pl.ds(a0 * APART + t, SUB, stride=APART), :] = y
        for b in range(blocks):
            bs = slice(b * BLOCK, (b + 1) * BLOCK)
            gated = q_ref[bs, src].astype(F32) * conv[b * APART : b * APART + BLOCK, :]
            gated_ref[bs, dst] = gated
            power_ref[bs, :] += gated * gated

    stored = l_ref.shape[0]
    rest(0, stored, lambda g: group(g, l_ref.at[g]))
    rest(stored, groups, lambda g: group(g, tail_ref.at[g - stored]))


def norm_kernel(off_ref, own_ref, other_ref, scale_ref, gain_ref, out_hbm, buf, sem):
    half = own_ref.shape[1]
    copies = []
    for ref, base in ((own_ref, off_ref[0] * half), (other_ref, (1 - off_ref[0]) * half)):
        for first in range(0, half, STORE):
            at = len(copies) * STORE
            for g in range(STORE // LANE):
                gain = gain_ref[0:1, lanes(base + first, g)]
                gated = ref[:, first + g * LANE : first + (g + 1) * LANE]
                buf[:, at + g * LANE : at + (g + 1) * LANE] = (gated * gain * scale_ref[...]).astype(buf.dtype)
            to = pl.ds(pl.multiple_of(base + first, LANE), STORE)
            copies.append(pltpu.make_async_copy(buf.at[:, at : at + STORE], out_hbm.at[:, to], sem.at[len(copies)]))
            copies[-1].start()
    for copy in copies:
        copy.wait()


def call(kernel, offset, ins, outs, far_outs, scratch, space=pltpu.VMEM, dtype=F32):
    return pl.pallas_call(
        kernel,
        in_specs=[pl.BlockSpec(memory_space=pltpu.SMEM)] + [pl.BlockSpec(memory_space=space)] * len(ins),
        out_specs=[pl.BlockSpec(memory_space=pltpu.VMEM)] * len(outs)
        + [pl.BlockSpec(memory_space=pltpu.HBM)] * len(far_outs),
        out_shape=[pltpu.VMEM(shape, dtype) for shape in outs] + [pltpu.HBM(shape, dtype) for shape in far_outs],
        scratch_shapes=scratch,
        compiler_params=pltpu.CompilerParams(vmem_limit_bytes=VMEM_LIMIT),
    )(offset, *[pltpu.with_memory_space_constraint(x, space) for x in ins])


def exchange(x, axis, distance):
    return lax.ppermute(x, axis, [(i, i ^ distance) for i in range(lax.axis_size(axis))])


def parts(x):
    half = x.shape[0] // 2
    return x[:half], x[half:]


def times(x, y):
    return jnp.concatenate(cmul(*parts(x), *parts(y)))


def per_device(q, k, v, decay, angle, res_r, res_i, skip_gain, norm_gain):
    rows, width = q.shape
    modes = decay.shape[0]
    half = width // 2
    blocks = rows // BLOCK
    count = lax.axis_size("seq")
    me = lax.axis_index("seq")
    upper = (me & 1) == 1
    own = (me & 1).astype(jnp.int32).reshape(1)
    other = 1 - own
    skip = skip_gain.reshape(1, width)
    gain = norm_gain.reshape(1, width)
    states = 2 * modes
    poles = (decay, angle, res_r, res_i)
    mixed = pltpu.VMEM((rows, LANE), F32)
    padded = pltpu.VMEM((blocks * APART, LANE), F32)
    state = (states, half)
    groups = half // LANE
    local = (groups - TAIL, blocks * states, LANE)
    tail = (TAIL, blocks * states, LANE)
    table = (groups, BLOCK * states, LANE)
    near_shape = (groups, rows, LANE)

    group_sem = pltpu.SemaphoreType.DMA((groups,))
    stored_sem = pltpu.SemaphoreType.DMA((groups - TAIL,))

    def near(offset, after, with_table):
        ins = [after, k, v, *poles, skip]
        tail_sem = pltpu.SemaphoreType.DMA((TAIL,))
        scratch = [mixed, padded, pltpu.VMEM(tail, F32), pltpu.VMEM(near_shape, F32), tail_sem, group_sem]
        return call(near_kernel, offset, ins, [table] * with_table, [tail, near_shape], scratch)

    def far(offset, start, local, tail, y, *ins):
        scratch = [pltpu.VMEM((blocks * (states + 1), LANE), F32), padded]
        outs = [(rows, half), (rows, LANE)] + [table] * (len(ins) > 1)
        return call(far_kernel, offset, [start, local, tail, y, q, *ins], outs, [], scratch)

    scratch = [
        pltpu.VMEM((rows, half), k.dtype),
        pltpu.VMEM((rows, half), v.dtype),
        pltpu.VMEM((4, modes, half), F32),
        mixed,
        pltpu.VMEM(local, F32),
        pltpu.SemaphoreType.DMA((2, half // FETCH)),
        pltpu.SemaphoreType.DMA((4,)),
        stored_sem,
    ]
    sent_end, sent_local = call(sent_kernel, other, [k, v, *poles], [state], [local], scratch, pltpu.HBM)
    pair_end = exchange(sent_end, "seq", 1)
    scratch = [mixed, pltpu.VMEM(local, F32), stored_sem]
    own_end, step_power, own_local = call(own_kernel, own, [k, v, *poles], [state] * 2, [local], scratch)
    low = jnp.where(upper, pair_end, own_end)
    high = jnp.where(upper, own_end, pair_end)
    total = times(step_power, low) + high
    before = mine = None
    jump = times(step_power, step_power)
    pending = [own, other]
    ready = []
    distance = 2
    while distance < count:
        got = exchange(total, "seq", distance)
        if pending:
            ready.append(near(pending.pop(0), total, bool(ready)))
            got, ready[-1] = lax.optimization_barrier((got, ready[-1]))
        above = (me & distance) != 0
        if before is None:
            before = jnp.where(above, got, 0.0)
            mine = jnp.concatenate([jnp.where(above, parts(jump)[0], 1.0), jnp.where(above, parts(jump)[1], 0.0)])
        else:
            before = jnp.where(above, before + times(mine, got), before)
            mine = jnp.where(above, times(mine, jump), mine)
        total = jnp.where(above, times(jump, got) + total, times(jump, total) + got)
        jump = times(jump, jump)
        distance *= 2
    for offset in pending:
        ready.append(near(offset, total, bool(ready)))
    after_low = times(step_power, before) + low
    own_start = jnp.where(upper, after_low, before)
    other_start = exchange(jnp.where(upper, before, after_low), "seq", 1)
    own_table, *other_ready = ready[1]
    own_gated, own_power, other_table = far(own, own_start, own_local, *ready[0], own_table, decay, angle)
    other_gated, other_power = far(other, other_start, sent_local, *other_ready, other_table)
    power = jnp.sum(own_power + other_power, axis=1)
    distance = 1
    while distance < lax.axis_size("ch"):
        power = power + exchange(power, "ch", distance)
        distance *= 2
    scale = lax.rsqrt(power / (width * lax.axis_size("ch")) + 1e-05)
    scale = jnp.broadcast_to(scale[:, None], (rows, LANE))
    scratch = [pltpu.VMEM((rows, width), jnp.bfloat16), pltpu.SemaphoreType.DMA((width // STORE,))]
    ins = [own_gated, other_gated, scale, gain]
    return call(norm_kernel, own, ins, [], [(rows, width)], scratch, dtype=jnp.bfloat16)[0]


def solution(mesh):
    rows = P("seq", "ch")
    poles = P(None, "ch")
    return jax.shard_map(
        per_device,
        mesh=mesh,
        in_specs=(rows, rows, rows, poles, poles, poles, poles, P("ch"), P("ch")),
        out_specs=rows,
        check_vma=False,
    )
```

```python
import functools

import jax
import jax.numpy as jnp
from jax import lax
from jax.experimental import pallas as pl
from jax.experimental.pallas import tpu as pltpu
from jax.sharding import PartitionSpec as P

F32 = jnp.float32
SUB = 8
LANE = 128
BLOCK = 16
APART = BLOCK + 1
FETCH = 128
STORE = 512
TAIL = 2
TOKENS = 8
VMEM_LIMIT = 8 * 2**20


def cmul(ar, ai, br, bi):
    return ar * br - ai * bi, ar * bi + ai * br


def cos_sin(r, n):
    z = r * r
    s = r + r * z * (-1.66666667e-1 + z * (8.33333310e-3 + z * (-1.98409296e-4 + z * 2.7181716e-6)))
    c = 1.0 + z * (-0.5 + z * (4.16666664e-2 + z * (-1.38888642e-3 + z * 2.4760495e-5)))
    quarter = n - 4.0 * jnp.floor(n * 0.25)
    odd = (quarter == 1.0) | (quarter == 3.0)
    sin = jnp.where(odd, c, s)
    cos = jnp.where(odd, s, c)
    sin = jnp.where(quarter >= 2.0, -sin, sin)
    cos = jnp.where((quarter == 1.0) | (quarter == 2.0), -cos, cos)
    return cos, sin


def pole_power(decay, angle, count):
    phase = angle * float(count)
    n = jnp.floor(phase * 0.6366197723675814 + 0.5)
    r = ((phase - n * 1.5703125) - n * 4.837512969970703125e-4) - n * 7.549789948768648e-8
    cos, sin = cos_sin(r, n)
    size = jnp.exp(decay * -float(count))
    return size * cos, size * sin


def power_table(pr, pi, first_r, first_i, count):
    tr, ti = [first_r], [first_i]
    for _ in range(count - 1):
        r, i = cmul(tr[-1], ti[-1], pr, pi)
        tr.append(r)
        ti.append(i)
    return tr, ti


def squared(r, i, times):
    for _ in range(times):
        r, i = r * r - i * i, (r + r) * i
    return r, i


def lanes(start, group):
    return pl.ds(pl.multiple_of(start + group * LANE, LANE), LANE)


def row(ref, index, ls):
    return jnp.broadcast_to(ref[index : index + 1, ls], (SUB, LANE))


def pole_table(a_ref, th_ref, rr_ref, ri_ref, ms, src):
    decay, angle = a_ref[ms, src], th_ref[ms, src]
    pr, pi = pole_power(decay, angle, 1)
    weight = jnp.sqrt(decay)
    return pr, pi, power_table(pr, pi, weight * rr_ref[ms, src], weight * ri_ref[ms, src], BLOCK)


def stream(groups, stores, body):
    def copies(g):
        return [pltpu.make_async_copy(buf.at[g], out.at[g], sem.at[g]) for buf, out, sem in stores]

    def fill(g, carry):
        body(g)
        for copy in copies(g):
            copy.start()
        return carry

    def finish(g, carry):
        for copy in copies(g):
            copy.wait()
        return carry

    lax.fori_loop(0, groups, fill, 0)
    return lambda: lax.fori_loop(0, groups, finish, 0)


def rest(start, stop, body):
    def step(g, carry):
        body(g)
        return carry

    lax.fori_loop(start, stop, step, 0)


def end_states(mixed, poles, at, e_ref, l_buf, pw_ref=None):
    a_ref, th_ref = poles[:2]
    rows = mixed.shape[0]
    modes = a_ref.shape[0]
    src, dst = at
    every = slice(None)
    starts = range(0, modes, SUB)
    tables, jump, state = {}, {}, {}
    for m0 in starts:
        ms = slice(m0, m0 + SUB)
        pr, pi, tables[m0] = pole_table(*poles, ms, src)
        jump[m0] = squared(pr, pi, BLOCK.bit_length() - 1)
        if pw_ref is not None:
            wr, wi = pole_power(a_ref[ms, src], th_ref[ms, src], rows)
            pw_ref[ms, dst] = wr
            pw_ref[modes + m0 : modes + m0 + SUB, dst] = wi
    for b in range(rows // BLOCK):
        enter = {}
        for s in range(BLOCK):
            x = row(mixed, b * BLOCK + s, every)
            for m0 in starts:
                r, i = tables[m0][0][BLOCK - 1 - s] * x, tables[m0][1][BLOCK - 1 - s] * x
                enter[m0] = (r, i) if s == 0 else (enter[m0][0] + r, enter[m0][1] + i)
        for m0 in starts:
            base = b * 2 * modes + m0
            if b == 0:
                state[m0] = enter[m0]
                continue
            sr, si = state[m0]
            if l_buf is not None:
                l_buf[base : base + SUB, :] = sr
                l_buf[base + modes : base + modes + SUB, :] = si
            sr, si = cmul(*jump[m0], sr, si)
            state[m0] = sr + enter[m0][0], si + enter[m0][1]
    if e_ref is not None:
        for m0 in starts:
            e_ref[m0 : m0 + SUB, dst], e_ref[modes + m0 : modes + m0 + SUB, dst] = state[m0]


def sent_kernel(off_ref, k_hbm, v_hbm, a_hbm, th_hbm, rr_hbm, ri_hbm, e_ref, l_hbm, kb, vb, pb, mixed, l_buf, kv_sem, p_sem, l_sem):
    half = e_ref.shape[1]
    base = off_ref[0] * half

    def fetches(c):
        first, size = ((0, FETCH), (FETCH, half - FETCH))[c]
        there = pl.ds(pl.multiple_of(base + first, LANE), size)
        return [
            pltpu.make_async_copy(src.at[:, there], dst.at[:, first : first + size], kv_sem.at[i, c])
            for i, (src, dst) in enumerate(((k_hbm, kb), (v_hbm, vb)))
        ]

    whole = pl.ds(pl.multiple_of(base, LANE), half)
    poles = [
        pltpu.make_async_copy(src.at[:, whole], pb.at[i], p_sem.at[i])
        for i, src in enumerate((a_hbm, th_hbm, rr_hbm, ri_hbm))
    ]
    for copy in poles + fetches(0) + fetches(1):
        copy.start()
    for copy in poles:
        copy.wait()

    def group(g, l_buf):
        for c in range(2):

            @pl.when(g == c * FETCH // LANE)
            def _():
                for copy in fetches(c):
                    copy.wait()

        ls = lanes(0, g)
        mixed[...] = kb[:, ls].astype(F32) * vb[:, ls].astype(F32)
        end_states(mixed, [pb.at[i] for i in range(4)], (ls, ls), e_ref, l_buf)

    stored = l_hbm.shape[0]
    finish = stream(stored, [(l_buf, l_hbm, l_sem)], lambda g: group(g, l_buf.at[g]))
    rest(stored, half // LANE, lambda g: group(g, None))
    finish()


def own_kernel(off_ref, k_ref, v_ref, a_ref, th_ref, rr_ref, ri_ref, e_ref, pw_ref, l_hbm, mixed, l_buf, l_sem):
    half = e_ref.shape[1]

    def group(g, l_buf):
        src, dst = lanes(off_ref[0] * half, g), lanes(0, g)
        mixed[...] = k_ref[:, src].astype(F32) * v_ref[:, src].astype(F32)
        end_states(mixed, (a_ref, th_ref, rr_ref, ri_ref), (src, dst), e_ref, l_buf, pw_ref)

    stored = l_hbm.shape[0]
    finish = stream(stored, [(l_buf, l_hbm, l_sem)], lambda g: group(g, l_buf.at[g]))
    rest(stored, half // LANE, lambda g: group(g, None))
    finish()


def fill_table(table, pr, pi, m0, modes):
    tr, ti = power_table(pr, pi, pr, pi, BLOCK)
    for j in range(BLOCK):
        base = j * 2 * modes + m0
        table[base : base + SUB, :] = tr[j]
        table[base + modes : base + modes + SUB, :] = ti[j]


def near_kernel(
    off_ref, after_ref, k_ref, v_ref, a_ref, th_ref, rr_ref, ri_ref, skip_ref, *refs
):
    if len(refs) > 8:
        table_ref, *refs = refs
    else:
        table_ref = None
    l_hbm, y_hbm, plain, mixed, l_buf, y_buf, l_sem, y_sem = refs
    rows = k_ref.shape[0]
    modes = a_ref.shape[0]
    groups = y_hbm.shape[0]
    half = groups * LANE
    blocks = rows // BLOCK

    def group(g):
        src = lanes(off_ref[0] * half, g)
        for b in range(blocks):
            bs = slice(b * BLOCK, (b + 1) * BLOCK)
            mixed[b * APART : b * APART + BLOCK, :] = k_ref[bs, src].astype(F32) * v_ref[bs, src].astype(F32)
        sums = None
        for m0 in range(0, modes, SUB):
            pr, pi, (tr, _) = pole_table(a_ref, th_ref, rr_ref, ri_ref, slice(m0, m0 + SUB), src)
            sums = tr if sums is None else [x + y for x, y in zip(sums, tr)]
            if table_ref is not None:
                ms, there = slice(m0, m0 + SUB), lanes((1 - off_ref[0]) * half, g)
                fill_table(table_ref.at[g], *pole_power(a_ref[ms, there], th_ref[ms, there], 1), m0, modes)
        taps = []
        for j in range(BLOCK):
            tap = jnp.sum(sums[j], axis=0, keepdims=True)
            if j == 0:
                tap = tap + skip_ref[0:1, src]
            taps.append(jnp.broadcast_to(tap, (SUB, LANE)))
        for a0 in range(0, blocks, SUB):
            acc = [None] * BLOCK
            for s in range(BLOCK):
                x = mixed[pl.ds(a0 * APART + s, SUB, stride=APART), :]
                for t in range(s, BLOCK):
                    part = taps[t - s] * x
                    acc[t] = part if acc[t] is None else acc[t] + part
            for t in range(BLOCK):
                y_buf[g, t * blocks + a0 : t * blocks + a0 + SUB, :] = acc[t]

    tail = l_hbm.shape[0]

    def states(i):
        src = lanes(off_ref[0] * half, groups - tail + i)
        plain[...] = k_ref[:, src].astype(F32) * v_ref[:, src].astype(F32)
        end_states(plain, (a_ref, th_ref, rr_ref, ri_ref), (src, src), None, l_buf.at[i])

    finish_states = stream(tail, [(l_buf, l_hbm, l_sem)], states)
    finish = stream(groups, [(y_buf, y_hbm, y_sem)], group)
    finish_states()
    finish()


def far_kernel(off_ref, s_ref, l_ref, tail_ref, y_ref, q_ref, table_ref, *refs):
    if len(refs) > 4:
        a_ref, th_ref, gated_ref, power_ref, next_ref, state, conv = refs
    else:
        gated_ref, power_ref, state, conv = refs
        next_ref = None
    rows = q_ref.shape[0]
    modes = s_ref.shape[0] // 2
    groups = y_ref.shape[0]
    half = groups * LANE
    blocks = rows // BLOCK
    starts = range(0, blocks, SUB)
    apart = 2 * modes + 1
    every = slice(None)
    power_ref[...] = jnp.zeros_like(power_ref)

    def group(g, l_ref):
        src, dst = lanes(off_ref[0] * half, g), lanes(0, g)
        table = table_ref.at[g]
        for m0 in range(0, modes, SUB):
            ms = slice(m0, m0 + SUB)
            if next_ref is not None:
                there = lanes((1 - off_ref[0]) * half, g)
                fill_table(next_ref.at[g], *pole_power(a_ref[ms, there], th_ref[ms, there], 1), m0, modes)
            last = (BLOCK - 1) * 2 * modes + m0
            qr, qi = table[last : last + SUB, :], table[last + modes : last + modes + SUB, :]
            sr, si = s_ref[ms, dst], s_ref[modes + m0 : modes + m0 + SUB, dst]
            for b in range(blocks):
                at = b * 2 * modes + m0
                to = b * apart + m0
                lr, li = (l_ref[at : at + SUB, :], l_ref[at + modes : at + modes + SUB, :]) if b else (0.0, 0.0)
                state[to : to + SUB, :] = lr + sr
                state[to + modes : to + modes + SUB, :] = li + si
                if b < blocks - 1:
                    sr, si = cmul(qr, qi, sr, si)
        for t0 in range(0, BLOCK, TOKENS):
            acc = {
                (t, a0): y_ref[g, t * blocks + a0 : t * blocks + a0 + SUB, :]
                for t in range(t0, t0 + TOKENS)
                for a0 in starts
            }
            for m in range(modes):
                cr = {a0: state[pl.ds(a0 * apart + m, SUB, stride=apart), :] for a0 in starts}
                ci = {a0: state[pl.ds(a0 * apart + modes + m, SUB, stride=apart), :] for a0 in starts}
                for t in range(t0, t0 + TOKENS):
                    br = row(table, t * 2 * modes + m, every)
                    bi = row(table, t * 2 * modes + modes + m, every)
                    for a0 in starts:
                        acc[t, a0] = acc[t, a0] + cr[a0] * br - ci[a0] * bi
            for (t, a0), y in acc.items():
                conv[pl.ds(a0 * APART + t, SUB, stride=APART), :] = y
        for b in range(blocks):
            bs = slice(b * BLOCK, (b + 1) * BLOCK)
            gated = q_ref[bs, src].astype(F32) * conv[b * APART : b * APART + BLOCK, :]
            gated_ref[bs, dst] = gated
            power_ref[bs, :] += gated * gated

    stored = l_ref.shape[0]
    rest(0, stored, lambda g: group(g, l_ref.at[g]))
    rest(stored, groups, lambda g: group(g, tail_ref.at[g - stored]))


def norm_kernel(off_ref, own_ref, other_ref, scale_ref, gain_ref, out_hbm, buf, sem):
    half = own_ref.shape[1]
    copies = []
    for ref, base in ((own_ref, off_ref[0] * half), (other_ref, (1 - off_ref[0]) * half)):
        for first in range(0, half, STORE):
            at = len(copies) * STORE
            for g in range(STORE // LANE):
                gain = gain_ref[0:1, lanes(base + first, g)]
                gated = ref[:, first + g * LANE : first + (g + 1) * LANE]
                buf[:, at + g * LANE : at + (g + 1) * LANE] = (gated * gain * scale_ref[...]).astype(buf.dtype)
            to = pl.ds(pl.multiple_of(base + first, LANE), STORE)
            copies.append(pltpu.make_async_copy(buf.at[:, at : at + STORE], out_hbm.at[:, to], sem.at[len(copies)]))
            copies[-1].start()
    for copy in copies:
        copy.wait()


def call(kernel, offset, ins, outs, far_outs, scratch, space=pltpu.VMEM, dtype=F32):
    return pl.pallas_call(
        kernel,
        in_specs=[pl.BlockSpec(memory_space=pltpu.SMEM)] + [pl.BlockSpec(memory_space=space)] * len(ins),
        out_specs=[pl.BlockSpec(memory_space=pltpu.VMEM)] * len(outs)
        + [pl.BlockSpec(memory_space=pltpu.HBM)] * len(far_outs),
        out_shape=[pltpu.VMEM(shape, dtype) for shape in outs] + [pltpu.HBM(shape, dtype) for shape in far_outs],
        scratch_shapes=scratch,
        compiler_params=pltpu.CompilerParams(vmem_limit_bytes=VMEM_LIMIT),
    )(offset, *[pltpu.with_memory_space_constraint(x, space) for x in ins])


def exchange(x, axis, distance):
    return lax.ppermute(x, axis, [(i, i ^ distance) for i in range(lax.axis_size(axis))])


def parts(x):
    half = x.shape[0] // 2
    return x[:half], x[half:]


def times(x, y):
    return jnp.concatenate(cmul(*parts(x), *parts(y)))


def per_device(q, k, v, decay, angle, res_r, res_i, skip_gain, norm_gain):
    rows, width = q.shape
    modes = decay.shape[0]
    half = width // 2
    blocks = rows // BLOCK
    count = lax.axis_size("seq")
    me = lax.axis_index("seq")
    upper = (me & 1) == 1
    own = (me & 1).astype(jnp.int32).reshape(1)
    other = 1 - own
    skip = skip_gain.reshape(1, width)
    gain = norm_gain.reshape(1, width)
    states = 2 * modes
    poles = (decay, angle, res_r, res_i)
    mixed = pltpu.VMEM((rows, LANE), F32)
    padded = pltpu.VMEM(((blocks + 1) * APART + SUB, LANE), F32)
    state = (states, half)
    groups = half // LANE
    local = (groups - TAIL, blocks * states, LANE)
    tail = (TAIL, blocks * states, LANE)
    table = (groups, BLOCK * states, LANE)
    near_shape = (groups, rows, LANE)

    group_sem = pltpu.SemaphoreType.DMA((groups,))
    stored_sem = pltpu.SemaphoreType.DMA((groups - TAIL,))

    def near(offset, after, with_table):
        ins = [after, k, v, *poles, skip]
        tail_sem = pltpu.SemaphoreType.DMA((TAIL,))
        scratch = [mixed, padded, pltpu.VMEM(tail, F32), pltpu.VMEM(near_shape, F32), tail_sem, group_sem]
        return call(near_kernel, offset, ins, [table] * with_table, [tail, near_shape], scratch)

    def far(offset, start, local, tail, y, *ins):
        scratch = [pltpu.VMEM(((blocks + 1) * (states + 1) + SUB, LANE), F32), padded]
        outs = [(rows, half), (rows, LANE)] + [table] * (len(ins) > 1)
        return call(far_kernel, offset, [start, local, tail, y, q, *ins], outs, [], scratch)

    scratch = [
        pltpu.VMEM((rows, half), k.dtype),
        pltpu.VMEM((rows, half), v.dtype),
        pltpu.VMEM((4, modes, half), F32),
        mixed,
        pltpu.VMEM(local, F32),
        pltpu.SemaphoreType.DMA((2, 2)),
        pltpu.SemaphoreType.DMA((4,)),
        stored_sem,
    ]
    sent_end, sent_local = call(sent_kernel, other, [k, v, *poles], [state], [local], scratch, pltpu.HBM)
    pair_end = exchange(sent_end, "seq", 1)
    scratch = [mixed, pltpu.VMEM(local, F32), stored_sem]
    own_end, step_power, own_local = call(own_kernel, own, [k, v, *poles], [state] * 2, [local], scratch)
    low = jnp.where(upper, pair_end, own_end)
    high = jnp.where(upper, own_end, pair_end)
    total = times(step_power, low) + high
    before = mine = None
    jump = times(step_power, step_power)
    pending = [own, other]
    ready = []
    distance = 2
    while distance < count:
        got = exchange(total, "seq", distance)
        if pending:
            ready.append(near(pending.pop(0), total, bool(ready)))
            got, ready[-1] = lax.optimization_barrier((got, ready[-1]))
        above = (me & distance) != 0
        if before is None:
            before = jnp.where(above, got, 0.0)
            mine = jnp.concatenate([jnp.where(above, parts(jump)[0], 1.0), jnp.where(above, parts(jump)[1], 0.0)])
        else:
            before = jnp.where(above, before + times(mine, got), before)
            mine = jnp.where(above, times(mine, jump), mine)
        total = jnp.where(above, times(jump, got) + total, times(jump, total) + got)
        jump = times(jump, jump)
        distance *= 2
    for offset in pending:
        ready.append(near(offset, total, bool(ready)))
    after_low = times(step_power, before) + low
    own_start = jnp.where(upper, after_low, before)
    other_start = exchange(jnp.where(upper, before, after_low), "seq", 1)
    own_table, *other_ready = ready[1]
    own_gated, own_power, other_table = far(own, own_start, own_local, *ready[0], own_table, decay, angle)
    other_gated, other_power = far(other, other_start, sent_local, *other_ready, other_table)
    power = jnp.sum(own_power + other_power, axis=1)
    distance = 1
    while distance < lax.axis_size("ch"):
        power = power + exchange(power, "ch", distance)
        distance *= 2
    scale = lax.rsqrt(power / (width * lax.axis_size("ch")) + 1e-05)
    scale = jnp.broadcast_to(scale[:, None], (rows, LANE))
    scratch = [pltpu.VMEM((rows, width), jnp.bfloat16), pltpu.SemaphoreType.DMA((width // STORE,))]
    ins = [own_gated, other_gated, scale, gain]
    return call(norm_kernel, own, ins, [], [(rows, width)], scratch, dtype=jnp.bfloat16)[0]


def solution(mesh):
    rows = P("seq", "ch")
    poles = P(None, "ch")
    return jax.shard_map(
        per_device,
        mesh=mesh,
        in_specs=(rows, rows, rows, poles, poles, poles, poles, P("ch"), P("ch")),
        out_specs=rows,
        check_vma=False,
    )
```

```python
import functools

import jax
import jax.numpy as jnp
from jax import lax
from jax.experimental import pallas as pl
from jax.experimental.pallas import tpu as pltpu
from jax.sharding import PartitionSpec as P

F32 = jnp.float32
SUB = 8
LANE = 128
BLOCK = 16
APART = BLOCK + 1
FETCH = 128
STORE = 512
TAIL = 2
TOKENS = 8
VMEM_LIMIT = 8 * 2**20


def cmul(ar, ai, br, bi):
    return ar * br - ai * bi, ar * bi + ai * br


def cos_sin(r, n):
    z = r * r
    s = r + r * z * (-1.66666667e-1 + z * (8.33333310e-3 + z * (-1.98409296e-4 + z * 2.7181716e-6)))
    c = 1.0 + z * (-0.5 + z * (4.16666664e-2 + z * (-1.38888642e-3 + z * 2.4760495e-5)))
    quarter = n - 4.0 * jnp.floor(n * 0.25)
    odd = (quarter == 1.0) | (quarter == 3.0)
    sin = jnp.where(odd, c, s)
    cos = jnp.where(odd, s, c)
    sin = jnp.where(quarter >= 2.0, -sin, sin)
    cos = jnp.where((quarter == 1.0) | (quarter == 2.0), -cos, cos)
    return cos, sin


def pole_power(decay, angle, count):
    phase = angle * float(count)
    n = jnp.floor(phase * 0.6366197723675814 + 0.5)
    r = ((phase - n * 1.5703125) - n * 4.837512969970703125e-4) - n * 7.549789948768648e-8
    cos, sin = cos_sin(r, n)
    size = jnp.exp(decay * -float(count))
    return size * cos, size * sin


def power_table(pr, pi, first_r, first_i, count):
    tr, ti = [first_r], [first_i]
    for _ in range(count - 1):
        r, i = cmul(tr[-1], ti[-1], pr, pi)
        tr.append(r)
        ti.append(i)
    return tr, ti


def squared(r, i, times):
    for _ in range(times):
        r, i = r * r - i * i, (r + r) * i
    return r, i


def lanes(start, group):
    return pl.ds(pl.multiple_of(start + group * LANE, LANE), LANE)


def row(ref, index, ls):
    return jnp.broadcast_to(ref[index : index + 1, ls], (SUB, LANE))


def pole_table(a_ref, th_ref, rr_ref, ri_ref, ms, src):
    decay, angle = a_ref[ms, src], th_ref[ms, src]
    pr, pi = pole_power(decay, angle, 1)
    weight = jnp.sqrt(decay)
    return pr, pi, power_table(pr, pi, weight * rr_ref[ms, src], weight * ri_ref[ms, src], BLOCK)


def stream(groups, stores, body):
    def copies(g):
        return [pltpu.make_async_copy(buf.at[g], out.at[g], sem.at[g]) for buf, out, sem in stores]

    def fill(g, carry):
        body(g)
        for copy in copies(g):
            copy.start()
        return carry

    def finish(g, carry):
        for copy in copies(g):
            copy.wait()
        return carry

    lax.fori_loop(0, groups, fill, 0)
    return lambda: lax.fori_loop(0, groups, finish, 0)


def rest(start, stop, body):
    def step(g, carry):
        body(g)
        return carry

    lax.fori_loop(start, stop, step, 0)


def end_states(mixed, poles, at, e_ref, l_buf, pw_ref=None):
    a_ref, th_ref = poles
    rows = mixed.shape[0]
    modes = a_ref.shape[0]
    src, dst = at
    every = slice(None)
    starts = range(0, modes, SUB)
    tables, jump, state = {}, {}, {}
    for m0 in starts:
        ms = slice(m0, m0 + SUB)
        pr, pi = pole_power(a_ref[ms, src], th_ref[ms, src], 1)
        tr, ti = tables[m0] = power_table(pr, pi, pr, pi, BLOCK)
        jump[m0] = tr[-1], ti[-1]
        if pw_ref is not None:
            wr, wi = pole_power(a_ref[ms, src], th_ref[ms, src], rows)
            pw_ref[ms, dst] = wr
            pw_ref[modes + m0 : modes + m0 + SUB, dst] = wi
    for b in range(rows // BLOCK):
        enter = {}
        for s in range(BLOCK):
            x = row(mixed, b * BLOCK + s, every)
            for m0 in starts:
                if s == BLOCK - 1:
                    enter[m0] = enter[m0][0] + x, enter[m0][1]
                    continue
                r, i = tables[m0][0][BLOCK - 2 - s] * x, tables[m0][1][BLOCK - 2 - s] * x
                enter[m0] = (r, i) if s == 0 else (enter[m0][0] + r, enter[m0][1] + i)
        for m0 in starts:
            base = b * 2 * modes + m0
            if b == 0:
                state[m0] = enter[m0]
                continue
            sr, si = state[m0]
            if l_buf is not None:
                l_buf[base : base + SUB, :] = sr
                l_buf[base + modes : base + modes + SUB, :] = si
            sr, si = cmul(*jump[m0], sr, si)
            state[m0] = sr + enter[m0][0], si + enter[m0][1]
    if e_ref is not None:
        for m0 in starts:
            e_ref[m0 : m0 + SUB, dst], e_ref[modes + m0 : modes + m0 + SUB, dst] = state[m0]


def sent_kernel(off_ref, k_hbm, v_hbm, a_hbm, th_hbm, e_ref, l_hbm, kb, vb, pb, mixed, l_buf, kv_sem, p_sem, l_sem):
    half = e_ref.shape[1]
    base = off_ref[0] * half

    def fetches(c):
        first, size = ((0, FETCH), (FETCH, half - FETCH))[c]
        there = pl.ds(pl.multiple_of(base + first, LANE), size)
        return [
            pltpu.make_async_copy(src.at[:, there], dst.at[:, first : first + size], kv_sem.at[i, c])
            for i, (src, dst) in enumerate(((k_hbm, kb), (v_hbm, vb)))
        ]

    whole = pl.ds(pl.multiple_of(base, LANE), half)
    poles = [
        pltpu.make_async_copy(src.at[:, whole], pb.at[i], p_sem.at[i])
        for i, src in enumerate((a_hbm, th_hbm))
    ]
    for copy in poles + fetches(0) + fetches(1):
        copy.start()
    for copy in poles:
        copy.wait()

    def group(g, l_buf):
        for c in range(2):

            @pl.when(g == c * FETCH // LANE)
            def _():
                for copy in fetches(c):
                    copy.wait()

        ls = lanes(0, g)
        mixed[...] = kb[:, ls].astype(F32) * vb[:, ls].astype(F32)
        end_states(mixed, [pb.at[i] for i in range(2)], (ls, ls), e_ref, l_buf)

    stored = l_hbm.shape[0]
    finish = stream(stored, [(l_buf, l_hbm, l_sem)], lambda g: group(g, l_buf.at[g]))
    rest(stored, half // LANE, lambda g: group(g, None))
    finish()


def own_kernel(off_ref, k_ref, v_ref, a_ref, th_ref, e_ref, pw_ref, l_hbm, mixed, l_buf, l_sem):
    half = e_ref.shape[1]

    def group(g, l_buf):
        src, dst = lanes(off_ref[0] * half, g), lanes(0, g)
        mixed[...] = k_ref[:, src].astype(F32) * v_ref[:, src].astype(F32)
        end_states(mixed, (a_ref, th_ref), (src, dst), e_ref, l_buf, pw_ref)

    stored = l_hbm.shape[0]
    finish = stream(stored, [(l_buf, l_hbm, l_sem)], lambda g: group(g, l_buf.at[g]))
    rest(stored, half // LANE, lambda g: group(g, None))
    finish()


def fill_table(table, poles, m0, src):
    modes = poles[0].shape[0]
    pr, pi, (tr, ti) = pole_table(*poles, slice(m0, m0 + SUB), src)
    tr, ti = power_table(pr, pi, tr[1], ti[1], BLOCK)
    qr, qi = squared(pr, pi, BLOCK.bit_length() - 1)
    for j, (r, i) in enumerate(zip(tr + [qr], ti + [qi])):
        base = j * 2 * modes + m0
        table[base : base + SUB, :] = r
        table[base + modes : base + modes + SUB, :] = i


def near_kernel(
    off_ref, after_ref, k_ref, v_ref, a_ref, th_ref, rr_ref, ri_ref, skip_ref, *refs
):
    if len(refs) > 8:
        table_ref, *refs = refs
    else:
        table_ref = None
    l_hbm, y_hbm, plain, mixed, l_buf, y_buf, l_sem, y_sem = refs
    rows = k_ref.shape[0]
    modes = a_ref.shape[0]
    groups = y_hbm.shape[0]
    half = groups * LANE
    blocks = rows // BLOCK

    def group(g):
        src = lanes(off_ref[0] * half, g)
        for b in range(blocks):
            bs = slice(b * BLOCK, (b + 1) * BLOCK)
            mixed[b * APART : b * APART + BLOCK, :] = k_ref[bs, src].astype(F32) * v_ref[bs, src].astype(F32)
        sums = None
        for m0 in range(0, modes, SUB):
            pr, pi, (tr, _) = pole_table(a_ref, th_ref, rr_ref, ri_ref, slice(m0, m0 + SUB), src)
            sums = tr if sums is None else [x + y for x, y in zip(sums, tr)]
            if table_ref is not None:
                there = lanes((1 - off_ref[0]) * half, g)
                fill_table(table_ref.at[g], (a_ref, th_ref, rr_ref, ri_ref), m0, there)
        taps = []
        for j in range(BLOCK):
            tap = jnp.sum(sums[j], axis=0, keepdims=True)
            if j == 0:
                tap = tap + skip_ref[0:1, src]
            taps.append(jnp.broadcast_to(tap, (SUB, LANE)))
        for a0 in range(0, blocks, SUB):
            acc = [None] * BLOCK
            for s in range(BLOCK):
                x = mixed[pl.ds(a0 * APART + s, SUB, stride=APART), :]
                for t in range(s, BLOCK):
                    part = taps[t - s] * x
                    acc[t] = part if acc[t] is None else acc[t] + part
            for t in range(BLOCK):
                y_buf[g, t * blocks + a0 : t * blocks + a0 + SUB, :] = acc[t]

    tail = l_hbm.shape[0]

    def states(i):
        src = lanes(off_ref[0] * half, groups - tail + i)
        plain[...] = k_ref[:, src].astype(F32) * v_ref[:, src].astype(F32)
        end_states(plain, (a_ref, th_ref), (src, src), None, l_buf.at[i])

    finish_states = stream(tail, [(l_buf, l_hbm, l_sem)], states)
    finish = stream(groups, [(y_buf, y_hbm, y_sem)], group)
    finish_states()
    finish()


def far_kernel(off_ref, s_ref, l_ref, tail_ref, y_ref, q_ref, table_ref, *refs):
    if len(refs) > 4:
        *poles, gated_ref, power_ref, next_ref, state, conv = refs
    else:
        gated_ref, power_ref, state, conv = refs
        next_ref = None
    rows = q_ref.shape[0]
    modes = s_ref.shape[0] // 2
    groups = y_ref.shape[0]
    half = groups * LANE
    blocks = rows // BLOCK
    starts = range(0, blocks, SUB)
    apart = 2 * modes + 1
    every = slice(None)
    power_ref[...] = jnp.zeros_like(power_ref)

    def group(g, l_ref):
        src, dst = lanes(off_ref[0] * half, g), lanes(0, g)
        table = table_ref.at[g]
        for m0 in range(0, modes, SUB):
            ms = slice(m0, m0 + SUB)
            if next_ref is not None:
                there = lanes((1 - off_ref[0]) * half, g)
                fill_table(next_ref.at[g], poles, m0, there)
            last = BLOCK * 2 * modes + m0
            qr, qi = table[last : last + SUB, :], table[last + modes : last + modes + SUB, :]
            sr, si = s_ref[ms, dst], s_ref[modes + m0 : modes + m0 + SUB, dst]
            for b in range(blocks):
                at = b * 2 * modes + m0
                to = b * apart + m0
                lr, li = (l_ref[at : at + SUB, :], l_ref[at + modes : at + modes + SUB, :]) if b else (0.0, 0.0)
                state[to : to + SUB, :] = lr + sr
                state[to + modes : to + modes + SUB, :] = li + si
                if b < blocks - 1:
                    sr, si = cmul(qr, qi, sr, si)
        for t0 in range(0, BLOCK, TOKENS):
            acc = {
                (t, a0): y_ref[g, t * blocks + a0 : t * blocks + a0 + SUB, :]
                for t in range(t0, t0 + TOKENS)
                for a0 in starts
            }
            for m in range(modes):
                cr = {a0: state[pl.ds(a0 * apart + m, SUB, stride=apart), :] for a0 in starts}
                ci = {a0: state[pl.ds(a0 * apart + modes + m, SUB, stride=apart), :] for a0 in starts}
                for t in range(t0, t0 + TOKENS):
                    br = row(table, t * 2 * modes + m, every)
                    bi = row(table, t * 2 * modes + modes + m, every)
                    for a0 in starts:
                        acc[t, a0] = acc[t, a0] + cr[a0] * br - ci[a0] * bi
            for (t, a0), y in acc.items():
                conv[pl.ds(a0 * APART + t, SUB, stride=APART), :] = y
        for b in range(blocks):
            bs = slice(b * BLOCK, (b + 1) * BLOCK)
            gated = q_ref[bs, src].astype(F32) * conv[b * APART : b * APART + BLOCK, :]
            gated_ref[bs, dst] = gated
            power_ref[bs, :] += gated * gated

    stored = l_ref.shape[0]
    rest(0, stored, lambda g: group(g, l_ref.at[g]))
    rest(stored, groups, lambda g: group(g, tail_ref.at[g - stored]))


def norm_kernel(off_ref, own_ref, other_ref, scale_ref, gain_ref, out_hbm, buf, sem):
    half = own_ref.shape[1]
    copies = []
    for ref, base in ((own_ref, off_ref[0] * half), (other_ref, (1 - off_ref[0]) * half)):
        for first in range(0, half, STORE):
            at = len(copies) * STORE
            for g in range(STORE // LANE):
                gain = gain_ref[0:1, lanes(base + first, g)]
                gated = ref[:, first + g * LANE : first + (g + 1) * LANE]
                buf[:, at + g * LANE : at + (g + 1) * LANE] = (gated * gain * scale_ref[...]).astype(buf.dtype)
            to = pl.ds(pl.multiple_of(base + first, LANE), STORE)
            copies.append(pltpu.make_async_copy(buf.at[:, at : at + STORE], out_hbm.at[:, to], sem.at[len(copies)]))
            copies[-1].start()
    for copy in copies:
        copy.wait()


def call(kernel, offset, ins, outs, far_outs, scratch, space=pltpu.VMEM, dtype=F32):
    return pl.pallas_call(
        kernel,
        in_specs=[pl.BlockSpec(memory_space=pltpu.SMEM)] + [pl.BlockSpec(memory_space=space)] * len(ins),
        out_specs=[pl.BlockSpec(memory_space=pltpu.VMEM)] * len(outs)
        + [pl.BlockSpec(memory_space=pltpu.HBM)] * len(far_outs),
        out_shape=[pltpu.VMEM(shape, dtype) for shape in outs] + [pltpu.HBM(shape, dtype) for shape in far_outs],
        scratch_shapes=scratch,
        compiler_params=pltpu.CompilerParams(vmem_limit_bytes=VMEM_LIMIT),
    )(offset, *[pltpu.with_memory_space_constraint(x, space) for x in ins])


def exchange(x, axis, distance):
    return lax.ppermute(x, axis, [(i, i ^ distance) for i in range(lax.axis_size(axis))])


def parts(x):
    half = x.shape[0] // 2
    return x[:half], x[half:]


def times(x, y):
    return jnp.concatenate(cmul(*parts(x), *parts(y)))


def per_device(q, k, v, decay, angle, res_r, res_i, skip_gain, norm_gain):
    rows, width = q.shape
    modes = decay.shape[0]
    half = width // 2
    blocks = rows // BLOCK
    count = lax.axis_size("seq")
    me = lax.axis_index("seq")
    upper = (me & 1) == 1
    own = (me & 1).astype(jnp.int32).reshape(1)
    other = 1 - own
    skip = skip_gain.reshape(1, width)
    gain = norm_gain.reshape(1, width)
    states = 2 * modes
    poles = (decay, angle, res_r, res_i)
    mixed = pltpu.VMEM((rows, LANE), F32)
    padded = pltpu.VMEM(((blocks + 1) * APART + SUB, LANE), F32)
    state = (states, half)
    groups = half // LANE
    local = (groups - TAIL, blocks * states, LANE)
    tail = (TAIL, blocks * states, LANE)
    table = (groups, (BLOCK + 1) * states, LANE)
    near_shape = (groups, rows, LANE)

    group_sem = pltpu.SemaphoreType.DMA((groups,))
    stored_sem = pltpu.SemaphoreType.DMA((groups - TAIL,))

    def near(offset, after, with_table):
        ins = [after, k, v, *poles, skip]
        tail_sem = pltpu.SemaphoreType.DMA((TAIL,))
        scratch = [mixed, padded, pltpu.VMEM(tail, F32), pltpu.VMEM(near_shape, F32), tail_sem, group_sem]
        return call(near_kernel, offset, ins, [table] * with_table, [tail, near_shape], scratch)

    def far(offset, start, local, tail, y, *ins):
        scratch = [pltpu.VMEM(((blocks + 1) * (states + 1) + SUB, LANE), F32), padded]
        outs = [(rows, half), (rows, LANE)] + [table] * (len(ins) > 1)
        return call(far_kernel, offset, [start, local, tail, y, q, *ins], outs, [], scratch)

    scratch = [
        pltpu.VMEM((rows, half), k.dtype),
        pltpu.VMEM((rows, half), v.dtype),
        pltpu.VMEM((2, modes, half), F32),
        mixed,
        pltpu.VMEM(local, F32),
        pltpu.SemaphoreType.DMA((2, 2)),
        pltpu.SemaphoreType.DMA((2,)),
        stored_sem,
    ]
    sent_end, sent_local = call(sent_kernel, other, [k, v, decay, angle], [state], [local], scratch, pltpu.HBM)
    pair_end = exchange(sent_end, "seq", 1)
    scratch = [mixed, pltpu.VMEM(local, F32), stored_sem]
    own_end, step_power, own_local = call(own_kernel, own, [k, v, decay, angle], [state] * 2, [local], scratch)
    low = jnp.where(upper, pair_end, own_end)
    high = jnp.where(upper, own_end, pair_end)
    total = times(step_power, low) + high
    before = mine = None
    jump = times(step_power, step_power)
    pending = [own, other]
    ready = []
    distance = 2
    while distance < count:
        got = exchange(total, "seq", distance)
        if pending:
            ready.append(near(pending.pop(0), total, bool(ready)))
            got, ready[-1] = lax.optimization_barrier((got, ready[-1]))
        above = (me & distance) != 0
        if before is None:
            before = jnp.where(above, got, 0.0)
            mine = jnp.concatenate([jnp.where(above, parts(jump)[0], 1.0), jnp.where(above, parts(jump)[1], 0.0)])
        else:
            before = jnp.where(above, before + times(mine, got), before)
            mine = jnp.where(above, times(mine, jump), mine)
        total = jnp.where(above, times(jump, got) + total, times(jump, total) + got)
        jump = times(jump, jump)
        distance *= 2
    for offset in pending:
        ready.append(near(offset, total, bool(ready)))
    after_low = times(step_power, before) + low
    own_start = jnp.where(upper, after_low, before)
    other_start = exchange(jnp.where(upper, before, after_low), "seq", 1)
    own_table, *other_ready = ready[1]
    own_gated, own_power, other_table = far(own, own_start, own_local, *ready[0], own_table, *poles)
    other_gated, other_power = far(other, other_start, sent_local, *other_ready, other_table)
    power = jnp.sum(own_power + other_power, axis=1)
    distance = 1
    while distance < lax.axis_size("ch"):
        power = power + exchange(power, "ch", distance)
        distance *= 2
    scale = lax.rsqrt(power / (width * lax.axis_size("ch")) + 1e-05)
    scale = jnp.broadcast_to(scale[:, None], (rows, LANE))
    scratch = [pltpu.VMEM((rows, width), jnp.bfloat16), pltpu.SemaphoreType.DMA((width // STORE,))]
    ins = [own_gated, other_gated, scale, gain]
    return call(norm_kernel, own, ins, [], [(rows, width)], scratch, dtype=jnp.bfloat16)[0]


def solution(mesh):
    rows = P("seq", "ch")
    poles = P(None, "ch")
    return jax.shard_map(
        per_device,
        mesh=mesh,
        in_specs=(rows, rows, rows, poles, poles, poles, poles, P("ch"), P("ch")),
        out_specs=rows,
        check_vma=False,
    )
```

```python
import functools

import jax
import jax.numpy as jnp
from jax import lax
from jax.experimental import pallas as pl
from jax.experimental.pallas import tpu as pltpu
from jax.sharding import PartitionSpec as P

F32 = jnp.float32
SUB = 8
LANE = 128
BLOCK = 16
APART = BLOCK + 1
FETCH = 128
STORE = 512
TAIL = 2
TOKENS = 8
VMEM_LIMIT = 8 * 2**20


def cmul(ar, ai, br, bi):
    return ar * br - ai * bi, ar * bi + ai * br


def cos_sin(r, n):
    z = r * r
    s = r + r * z * (-1.66666667e-1 + z * (8.33333310e-3 + z * (-1.98409296e-4 + z * 2.7181716e-6)))
    c = 1.0 + z * (-0.5 + z * (4.16666664e-2 + z * (-1.38888642e-3 + z * 2.4760495e-5)))
    quarter = n - 4.0 * jnp.floor(n * 0.25)
    odd = (quarter == 1.0) | (quarter == 3.0)
    sin = jnp.where(odd, c, s)
    cos = jnp.where(odd, s, c)
    sin = jnp.where(quarter >= 2.0, -sin, sin)
    cos = jnp.where((quarter == 1.0) | (quarter == 2.0), -cos, cos)
    return cos, sin


def pole_power(decay, angle, count):
    phase = angle * float(count)
    n = jnp.floor(phase * 0.6366197723675814 + 0.5)
    if count == 1:
        r = (phase - n * 1.57079637050628662109375) + n * 4.37113900018624283e-8
    else:
        r = ((phase - n * 1.5703125) - n * 4.837512969970703125e-4) - n * 7.549789948768648e-8
    cos, sin = cos_sin(r, n)
    size = jnp.exp(decay * -float(count))
    return size * cos, size * sin


def power_table(pr, pi, first_r, first_i, count):
    tr, ti = [first_r], [first_i]
    for _ in range(count - 1):
        r, i = cmul(tr[-1], ti[-1], pr, pi)
        tr.append(r)
        ti.append(i)
    return tr, ti


def squared(r, i, times):
    for _ in range(times):
        r, i = r * r - i * i, (r + r) * i
    return r, i


def lanes(start, group):
    return pl.ds(pl.multiple_of(start + group * LANE, LANE), LANE)


def row(ref, index, ls):
    return jnp.broadcast_to(ref[index : index + 1, ls], (SUB, LANE))


def pole_table(a_ref, th_ref, rr_ref, ri_ref, ms, src):
    decay, angle = a_ref[ms, src], th_ref[ms, src]
    pr, pi = pole_power(decay, angle, 1)
    weight = jnp.sqrt(decay)
    return pr, pi, power_table(pr, pi, weight * rr_ref[ms, src], weight * ri_ref[ms, src], BLOCK)


def stream(groups, stores, body):
    def copies(g):
        return [pltpu.make_async_copy(buf.at[g], out.at[g], sem.at[g]) for buf, out, sem in stores]

    def fill(g, carry):
        body(g)
        for copy in copies(g):
            copy.start()
        return carry

    def finish(g, carry):
        for copy in copies(g):
            copy.wait()
        return carry

    lax.fori_loop(0, groups, fill, 0)
    return lambda: lax.fori_loop(0, groups, finish, 0)


def rest(start, stop, body):
    def step(g, carry):
        body(g)
        return carry

    lax.fori_loop(start, stop, step, 0)


def end_states(mixed, poles, at, e_ref, l_buf, pw_ref=None):
    a_ref, th_ref = poles
    rows = mixed.shape[0]
    modes = a_ref.shape[0]
    src, dst = at
    every = slice(None)
    starts = range(0, modes, SUB)
    tables, jump, state = {}, {}, {}
    for m0 in starts:
        ms = slice(m0, m0 + SUB)
        pr, pi = pole_power(a_ref[ms, src], th_ref[ms, src], 1)
        tr, ti = tables[m0] = power_table(pr, pi, pr, pi, BLOCK)
        jump[m0] = tr[-1], ti[-1]
        if pw_ref is not None:
            wr, wi = pole_power(a_ref[ms, src], th_ref[ms, src], rows)
            pw_ref[ms, dst] = wr
            pw_ref[modes + m0 : modes + m0 + SUB, dst] = wi
    for b in range(rows // BLOCK):
        enter = {}
        for s in range(BLOCK):
            x = row(mixed, b * BLOCK + s, every)
            for m0 in starts:
                if s == BLOCK - 1:
                    enter[m0] = enter[m0][0] + x, enter[m0][1]
                    continue
                r, i = tables[m0][0][BLOCK - 2 - s] * x, tables[m0][1][BLOCK - 2 - s] * x
                enter[m0] = (r, i) if s == 0 else (enter[m0][0] + r, enter[m0][1] + i)
        for m0 in starts:
            base = b * 2 * modes + m0
            if b == 0:
                state[m0] = enter[m0]
                continue
            sr, si = state[m0]
            if l_buf is not None:
                l_buf[base : base + SUB, :] = sr
                l_buf[base + modes : base + modes + SUB, :] = si
            sr, si = cmul(*jump[m0], sr, si)
            state[m0] = sr + enter[m0][0], si + enter[m0][1]
    if e_ref is not None:
        for m0 in starts:
            e_ref[m0 : m0 + SUB, dst], e_ref[modes + m0 : modes + m0 + SUB, dst] = state[m0]


def sent_kernel(off_ref, k_hbm, v_hbm, a_hbm, th_hbm, e_ref, l_hbm, kb, vb, pb, mixed, l_buf, kv_sem, p_sem, l_sem):
    half = e_ref.shape[1]
    base = off_ref[0] * half

    def fetches(c):
        first, size = ((0, FETCH), (FETCH, half - FETCH))[c]
        there = pl.ds(pl.multiple_of(base + first, LANE), size)
        return [
            pltpu.make_async_copy(src.at[:, there], dst.at[:, first : first + size], kv_sem.at[i, c])
            for i, (src, dst) in enumerate(((k_hbm, kb), (v_hbm, vb)))
        ]

    whole = pl.ds(pl.multiple_of(base, LANE), half)
    poles = [
        pltpu.make_async_copy(src.at[:, whole], pb.at[i], p_sem.at[i])
        for i, src in enumerate((a_hbm, th_hbm))
    ]
    for copy in poles + fetches(0) + fetches(1):
        copy.start()
    for copy in poles:
        copy.wait()

    def group(g, l_buf):
        for c in range(2):

            @pl.when(g == c * FETCH // LANE)
            def _():
                for copy in fetches(c):
                    copy.wait()

        ls = lanes(0, g)
        mixed[...] = kb[:, ls].astype(F32) * vb[:, ls].astype(F32)
        end_states(mixed, [pb.at[i] for i in range(2)], (ls, ls), e_ref, l_buf)

    stored = l_hbm.shape[0]
    finish = stream(stored, [(l_buf, l_hbm, l_sem)], lambda g: group(g, l_buf.at[g]))
    rest(stored, half // LANE, lambda g: group(g, None))
    finish()


def own_kernel(off_ref, k_ref, v_ref, a_ref, th_ref, e_ref, pw_ref, l_hbm, mixed, l_buf, l_sem):
    half = e_ref.shape[1]

    def group(g, l_buf):
        src, dst = lanes(off_ref[0] * half, g), lanes(0, g)
        mixed[...] = k_ref[:, src].astype(F32) * v_ref[:, src].astype(F32)
        end_states(mixed, (a_ref, th_ref), (src, dst), e_ref, l_buf, pw_ref)

    stored = l_hbm.shape[0]
    finish = stream(stored, [(l_buf, l_hbm, l_sem)], lambda g: group(g, l_buf.at[g]))
    rest(stored, half // LANE, lambda g: group(g, None))
    finish()


def fill_table(table, poles, m0, src):
    modes = poles[0].shape[0]
    pr, pi, (tr, ti) = pole_table(*poles, slice(m0, m0 + SUB), src)
    tr, ti = power_table(pr, pi, tr[1], ti[1], BLOCK)
    qr, qi = squared(pr, pi, BLOCK.bit_length() - 1)
    for j, (r, i) in enumerate(zip(tr + [qr], ti + [qi])):
        base = j * 2 * modes + m0
        table[base : base + SUB, :] = r
        table[base + modes : base + modes + SUB, :] = i


def near_kernel(
    off_ref, after_ref, k_ref, v_ref, a_ref, th_ref, rr_ref, ri_ref, skip_ref, *refs
):
    if len(refs) > 8:
        table_ref, *refs = refs
    else:
        table_ref = None
    l_hbm, y_hbm, plain, mixed, l_buf, y_buf, l_sem, y_sem = refs
    rows = k_ref.shape[0]
    modes = a_ref.shape[0]
    groups = y_hbm.shape[0]
    half = groups * LANE
    blocks = rows // BLOCK

    def group(g):
        src = lanes(off_ref[0] * half, g)
        for b in range(blocks):
            bs = slice(b * BLOCK, (b + 1) * BLOCK)
            mixed[b * APART : b * APART + BLOCK, :] = k_ref[bs, src].astype(F32) * v_ref[bs, src].astype(F32)
        sums = None
        for m0 in range(0, modes, SUB):
            pr, pi, (tr, _) = pole_table(a_ref, th_ref, rr_ref, ri_ref, slice(m0, m0 + SUB), src)
            sums = tr if sums is None else [x + y for x, y in zip(sums, tr)]
            if table_ref is not None:
                there = lanes((1 - off_ref[0]) * half, g)
                fill_table(table_ref.at[g], (a_ref, th_ref, rr_ref, ri_ref), m0, there)
        taps = []
        for j in range(BLOCK):
            tap = jnp.sum(sums[j], axis=0, keepdims=True)
            if j == 0:
                tap = tap + skip_ref[0:1, src]
            taps.append(jnp.broadcast_to(tap, (SUB, LANE)))
        for a0 in range(0, blocks, SUB):
            acc = [None] * BLOCK
            for s in range(BLOCK):
                x = mixed[pl.ds(a0 * APART + s, SUB, stride=APART), :]
                for t in range(s, BLOCK):
                    part = taps[t - s] * x
                    acc[t] = part if acc[t] is None else acc[t] + part
            for t in range(BLOCK):
                y_buf[g, t * blocks + a0 : t * blocks + a0 + SUB, :] = acc[t]

    tail = l_hbm.shape[0]

    def states(i):
        src = lanes(off_ref[0] * half, groups - tail + i)
        plain[...] = k_ref[:, src].astype(F32) * v_ref[:, src].astype(F32)
        end_states(plain, (a_ref, th_ref), (src, src), None, l_buf.at[i])

    finish_states = stream(tail, [(l_buf, l_hbm, l_sem)], states)
    finish = stream(groups, [(y_buf, y_hbm, y_sem)], group)
    finish_states()
    finish()


def far_kernel(off_ref, s_ref, l_ref, tail_ref, y_ref, q_ref, table_ref, *refs):
    first_power = None
    if len(refs) > 5:
        *poles, gated_ref, power_ref, next_ref, state, conv = refs
    else:
        first_power, gated_ref, power_ref, state, conv = refs
        next_ref = None
    rows = q_ref.shape[0]
    modes = s_ref.shape[0] // 2
    groups = y_ref.shape[0]
    half = groups * LANE
    blocks = rows // BLOCK
    starts = range(0, blocks, SUB)
    apart = 2 * modes + 1
    every = slice(None)
    power_ref[...] = jnp.zeros_like(power_ref) if first_power is None else first_power[...]

    def group(g, l_ref):
        src, dst = lanes(off_ref[0] * half, g), lanes(0, g)
        table = table_ref.at[g]
        for m0 in range(0, modes, SUB):
            ms = slice(m0, m0 + SUB)
            if next_ref is not None:
                there = lanes((1 - off_ref[0]) * half, g)
                fill_table(next_ref.at[g], poles, m0, there)
            last = BLOCK * 2 * modes + m0
            qr, qi = table[last : last + SUB, :], table[last + modes : last + modes + SUB, :]
            sr, si = s_ref[ms, dst], s_ref[modes + m0 : modes + m0 + SUB, dst]
            for b in range(blocks):
                at = b * 2 * modes + m0
                to = b * apart + m0
                lr, li = (l_ref[at : at + SUB, :], l_ref[at + modes : at + modes + SUB, :]) if b else (0.0, 0.0)
                state[to : to + SUB, :] = lr + sr
                state[to + modes : to + modes + SUB, :] = li + si
                if b < blocks - 1:
                    sr, si = cmul(qr, qi, sr, si)
        for t0 in range(0, BLOCK, TOKENS):
            acc = {
                (t, a0): y_ref[g, t * blocks + a0 : t * blocks + a0 + SUB, :]
                for t in range(t0, t0 + TOKENS)
                for a0 in starts
            }
            for m in range(modes):
                cr = {a0: state[pl.ds(a0 * apart + m, SUB, stride=apart), :] for a0 in starts}
                ci = {a0: state[pl.ds(a0 * apart + modes + m, SUB, stride=apart), :] for a0 in starts}
                for t in range(t0, t0 + TOKENS):
                    br = row(table, t * 2 * modes + m, every)
                    bi = row(table, t * 2 * modes + modes + m, every)
                    for a0 in starts:
                        acc[t, a0] = acc[t, a0] + cr[a0] * br - ci[a0] * bi
            for (t, a0), y in acc.items():
                conv[pl.ds(a0 * APART + t, SUB, stride=APART), :] = y
        for b in range(blocks):
            bs = slice(b * BLOCK, (b + 1) * BLOCK)
            gated = q_ref[bs, src].astype(F32) * conv[b * APART : b * APART + BLOCK, :]
            gated_ref[bs, dst] = gated
            power_ref[bs, :] += gated * gated

    stored = l_ref.shape[0]
    rest(0, stored, lambda g: group(g, l_ref.at[g]))
    rest(stored, groups, lambda g: group(g, tail_ref.at[g - stored]))


def norm_kernel(off_ref, own_ref, other_ref, scale_ref, gain_ref, out_hbm, buf, sem):
    half = own_ref.shape[1]
    copies = []
    for ref, base in ((own_ref, off_ref[0] * half), (other_ref, (1 - off_ref[0]) * half)):
        for first in range(0, half, STORE):
            at = len(copies) * STORE
            for g in range(STORE // LANE):
                gain = gain_ref[0:1, lanes(base + first, g)]
                gated = ref[:, first + g * LANE : first + (g + 1) * LANE]
                buf[:, at + g * LANE : at + (g + 1) * LANE] = (gated * gain * scale_ref[...]).astype(buf.dtype)
            to = pl.ds(pl.multiple_of(base + first, LANE), STORE)
            copies.append(pltpu.make_async_copy(buf.at[:, at : at + STORE], out_hbm.at[:, to], sem.at[len(copies)]))
            copies[-1].start()
    for copy in copies:
        copy.wait()


def call(kernel, offset, ins, outs, far_outs, scratch, space=pltpu.VMEM, dtype=F32):
    return pl.pallas_call(
        kernel,
        in_specs=[pl.BlockSpec(memory_space=pltpu.SMEM)] + [pl.BlockSpec(memory_space=space)] * len(ins),
        out_specs=[pl.BlockSpec(memory_space=pltpu.VMEM)] * len(outs)
        + [pl.BlockSpec(memory_space=pltpu.HBM)] * len(far_outs),
        out_shape=[pltpu.VMEM(shape, dtype) for shape in outs] + [pltpu.HBM(shape, dtype) for shape in far_outs],
        scratch_shapes=scratch,
        compiler_params=pltpu.CompilerParams(vmem_limit_bytes=VMEM_LIMIT),
    )(offset, *[pltpu.with_memory_space_constraint(x, space) for x in ins])


def exchange(x, axis, distance):
    return lax.ppermute(x, axis, [(i, i ^ distance) for i in range(lax.axis_size(axis))])


def parts(x):
    half = x.shape[0] // 2
    return x[:half], x[half:]


def times(x, y):
    return jnp.concatenate(cmul(*parts(x), *parts(y)))


def per_device(q, k, v, decay, angle, res_r, res_i, skip_gain, norm_gain):
    rows, width = q.shape
    modes = decay.shape[0]
    half = width // 2
    blocks = rows // BLOCK
    count = lax.axis_size("seq")
    me = lax.axis_index("seq")
    upper = (me & 1) == 1
    own = (me & 1).astype(jnp.int32).reshape(1)
    other = 1 - own
    skip = skip_gain.reshape(1, width)
    gain = norm_gain.reshape(1, width)
    states = 2 * modes
    poles = (decay, angle, res_r, res_i)
    mixed = pltpu.VMEM((rows, LANE), F32)
    padded = pltpu.VMEM(((blocks + 1) * APART + SUB, LANE), F32)
    state = (states, half)
    groups = half // LANE
    local = (groups - TAIL, blocks * states, LANE)
    tail = (TAIL, blocks * states, LANE)
    table = (groups, (BLOCK + 1) * states, LANE)
    near_shape = (groups, rows, LANE)

    group_sem = pltpu.SemaphoreType.DMA((groups,))
    stored_sem = pltpu.SemaphoreType.DMA((groups - TAIL,))

    def near(offset, after, with_table):
        ins = [after, k, v, *poles, skip]
        tail_sem = pltpu.SemaphoreType.DMA((TAIL,))
        scratch = [mixed, padded, pltpu.VMEM(tail, F32), pltpu.VMEM(near_shape, F32), tail_sem, group_sem]
        return call(near_kernel, offset, ins, [table] * with_table, [tail, near_shape], scratch)

    def far(offset, start, local, tail, y, *ins):
        scratch = [pltpu.VMEM(((blocks + 1) * (states + 1) + SUB, LANE), F32), padded]
        outs = [(rows, half), (rows, LANE)] + [table] * (len(ins) > 2)
        return call(far_kernel, offset, [start, local, tail, y, q, *ins], outs, [], scratch)

    scratch = [
        pltpu.VMEM((rows, half), k.dtype),
        pltpu.VMEM((rows, half), v.dtype),
        pltpu.VMEM((2, modes, half), F32),
        mixed,
        pltpu.VMEM(local, F32),
        pltpu.SemaphoreType.DMA((2, 2)),
        pltpu.SemaphoreType.DMA((2,)),
        stored_sem,
    ]
    sent_end, sent_local = call(sent_kernel, other, [k, v, decay, angle], [state], [local], scratch, pltpu.HBM)
    pair_end = exchange(sent_end, "seq", 1)
    scratch = [mixed, pltpu.VMEM(local, F32), stored_sem]
    own_end, step_power, own_local = call(own_kernel, own, [k, v, decay, angle], [state] * 2, [local], scratch)
    low = jnp.where(upper, pair_end, own_end)
    high = jnp.where(upper, own_end, pair_end)
    total = times(step_power, low) + high
    before = mine = None
    jump = times(step_power, step_power)
    pending = [own, other]
    ready = []
    distance = 2
    while distance < count:
        got = exchange(total, "seq", distance)
        if pending:
            ready.append(near(pending.pop(0), total, bool(ready)))
            got, ready[-1] = lax.optimization_barrier((got, ready[-1]))
        above = (me & distance) != 0
        if before is None:
            before = jnp.where(above, got, 0.0)
            mine = jnp.concatenate([jnp.where(above, parts(jump)[0], 1.0), jnp.where(above, parts(jump)[1], 0.0)])
        else:
            before = jnp.where(above, before + times(mine, got), before)
            mine = jnp.where(above, times(mine, jump), mine)
        total = jnp.where(above, times(jump, got) + total, times(jump, total) + got)
        jump = times(jump, jump)
        distance *= 2
    for offset in pending:
        ready.append(near(offset, total, bool(ready)))
    after_low = times(step_power, before) + low
    own_start = jnp.where(upper, after_low, before)
    other_start = exchange(jnp.where(upper, before, after_low), "seq", 1)
    own_table, *other_ready = ready[1]
    own_gated, own_power, other_table = far(own, own_start, own_local, *ready[0], own_table, *poles)
    other_gated, power = far(other, other_start, sent_local, *other_ready, other_table, own_power)
    power = jnp.sum(power, axis=1)
    distance = 1
    while distance < lax.axis_size("ch"):
        power = power + exchange(power, "ch", distance)
        distance *= 2
    scale = lax.rsqrt(power / (width * lax.axis_size("ch")) + 1e-05)
    scale = jnp.broadcast_to(scale[:, None], (rows, LANE))
    scratch = [pltpu.VMEM((rows, width), jnp.bfloat16), pltpu.SemaphoreType.DMA((width // STORE,))]
    ins = [own_gated, other_gated, scale, gain]
    return call(norm_kernel, own, ins, [], [(rows, width)], scratch, dtype=jnp.bfloat16)[0]


def solution(mesh):
    rows = P("seq", "ch")
    poles = P(None, "ch")
    return jax.shard_map(
        per_device,
        mesh=mesh,
        in_specs=(rows, rows, rows, poles, poles, poles, poles, P("ch"), P("ch")),
        out_specs=rows,
        check_vma=False,
    )
```
